512 devices in a mesh: dp: 16 (over y, z_lo), vocab: 32 (over x, z_hi, core).
Axes of the slice: x: 4, y: 8, z: 8 (z_hi: 4, z_lo: 2; z = z_hi * 2 + z_lo), core: 2. Of those that a mesh axis runs over, the one named last changes fastest.
Arguments:
- hidden: bfloat16 [2048, 3072], P('dp')
- head: bfloat16 [16, 8192, 3072], P('dp', 'vocab')
- teacher: bfloat16 [2048, 131072], P('dp', 'vocab')
- shard_order: int32 [32], replicated, may hold values from 0 to 31, each once
- loss_weight: float32 [2048], replicated, may hold values from 256 to 2048
Outputs:
- head_grad: bfloat16 [16, 8192, 3072], P('dp', 'vocab')
- divergence: float32 [2048], replicated
The draws below stay inside these ranges and needn't reach their ends.
Inputs may be any that keep to these rules, and one draw needn't show every extreme that they name: `shard_order`: each block number appears once.
All inputs are finite; a program needn't handle non-finite values.
Results may differ from the reference program's by a relative error of at most 0.0048.
Values may be sent and summed in bfloat16 or wider, within the bound.
A program may use at most 128 MiB of HBM per device.

```python
import math
import jax
import jax.numpy as jnp
from jax import lax

D = 3072
VOC_DEV = 4096
TOKENS = 2048
V = 131072
SUB = 256
HEAD_ROWS = 8192
N_DP = 16
N_VOCAB = 32


def head_base(key):
    return jax.random.normal(key, (N_DP, V // N_DP, D), jnp.float32)


def draw_head(key, part):
    base_rows = head_base(key)
    return (base_rows * (1.0 / jnp.sqrt(jnp.float32(D)))).astype(jnp.bfloat16)


def draw_hidden(key, part):
    key = jax.random.fold_in(key, 2)
    return jnp.clip(jax.random.normal(key, (TOKENS, D), jnp.float32), -6.0, 6.0).astype(jnp.bfloat16)


def draw_teacher(key, part):
    key = jax.random.fold_in(key, 3)
    keys = jax.random.split(key, 1)
    values = jax.random.normal(keys[0], (TOKENS, V), jnp.float32)
    return jnp.clip(values, -6.0, 6.0).astype(jnp.bfloat16)


def setup_inputs(seed: int = 0) -> dict:
    arg_keys = jax.random.split(jax.random.key(seed), 6)
    return {
        "hidden": draw_hidden(jax.random.fold_in(arg_keys[5], 71), 0),
        "head": draw_head(jax.random.fold_in(arg_keys[5], 71), 0),
        "teacher": draw_teacher(jax.random.fold_in(arg_keys[5], 71), 0),
        "shard_order": jax.random.permutation(arg_keys[3], N_VOCAB).astype(jnp.int32),
        "loss_weight": jnp.clip(jnp.exp(jax.random.uniform(arg_keys[4], (TOKENS,), jnp.float32, math.log(256.0), math.log(2048.0))), 256.0, 2048.0),
    }


def reference(hidden, head, teacher, shard_order, loss_weight):
    table = head.reshape(N_DP, N_VOCAB, SUB, D).transpose(1, 0, 2, 3).reshape(N_VOCAB, VOC_DEV, D)
    ordinal = jnp.arange(N_VOCAB, dtype=jnp.int32)
    matches = (shard_order[None, :] == ordinal[:, None]).astype(jnp.int32)
    inverse = lax.optimization_barrier(jnp.sum(matches * ordinal[None, :], axis=1)).astype(jnp.int32)
    blocks = teacher.reshape(TOKENS, N_VOCAB, VOC_DEV)

    def block_target(block_id):
        return lax.dynamic_index_in_dim(blocks, inverse[block_id], 1, keepdims=False).astype(jnp.float32)

    def gather_stats(running, block_id):
        top_s, sum_s, top_t, sum_t, cross = running
        rows = lax.dynamic_index_in_dim(table, block_id, 0, keepdims=False)
        scores = lax.dot_general(hidden, rows, (((1,), (1,)), ((), ())), preferred_element_type=jnp.float32)
        target = block_target(block_id)
        next_s = jnp.maximum(top_s, lax.optimization_barrier(jnp.max(scores, axis=1)))
        next_t = jnp.maximum(top_t, lax.optimization_barrier(jnp.max(target, axis=1)))
        sum_s = sum_s * jnp.exp(top_s - next_s) + lax.optimization_barrier(jnp.sum(jnp.exp(scores - next_s[:, None]), axis=1))
        exp_t = jnp.exp(target - next_t[:, None])
        factor = jnp.exp(top_t - next_t)
        sum_t = sum_t * factor + lax.optimization_barrier(jnp.sum(exp_t, axis=1))
        cross = cross * factor + lax.optimization_barrier(jnp.sum(exp_t * (target - scores), axis=1))
        return ((next_s, sum_s, next_t, sum_t, cross), scores)
    lowest = jnp.full((TOKENS,), -jnp.inf, jnp.float32)
    nothing = jnp.zeros((TOKENS,), jnp.float32)
    start = (lowest, nothing, lowest, nothing, nothing)
    (top_s, sum_s, top_t, sum_t, cross), scores = lax.scan(gather_stats, start, ordinal)
    divergence = cross / sum_t - top_t - jnp.log(sum_t) + top_s + jnp.log(sum_s)

    def block_grad(inputs):
        block_scores, block_id = inputs
        target = block_target(block_id)
        prob_s = jnp.exp(block_scores - top_s[:, None]) / sum_s[:, None]
        prob_t = jnp.exp(target - top_t[:, None]) / sum_t[:, None]
        logit_grad = (loss_weight[:, None] * (prob_s - prob_t)).astype(jnp.bfloat16)
        result = lax.dot_general(logit_grad, hidden, (((0,), (0,)), ((), ())), preferred_element_type=jnp.float32)
        return result.astype(jnp.bfloat16)
    grads = lax.map(block_grad, (scores, ordinal))
    head_grad = grads.reshape(N_VOCAB, N_DP, SUB, D).transpose(1, 0, 2, 3).reshape(N_DP, HEAD_ROWS, D)
    return (head_grad, divergence)
```

```python
import functools

import jax
import jax.numpy as jnp
from jax import lax
from jax.experimental import pallas as pl
from jax.experimental.pallas import tpu as pltpu
from jax.sharding import PartitionSpec as P

F32 = jnp.float32
BF16 = jnp.bfloat16
MESH = pl.DeviceIdType.MESH
SUB = 256


def kernel(
    nx, ny, nzh,
    inv_ref, hidden_ref, head_hbm, teacher_hbm, weight_ref,
    grad_ref, div_ref,
    hid, head, tv, tt, rr, qq, ww, tgt, sc, ex, pr,
    src1, ar1, tile2, ar2, tile3, fin, tst,
    csrc1, car1, ctile2, car2, ctile3, cfin,
    loc, zs, zr, ys, yr, xs, xr, cs, cr, t1s, t1r, t2s, t2r, t3s, t3r, as_, ar_,
):
    half = ny // 2
    n_dp = 2 * ny
    n_v = 2 * nx * nzh
    d_model = hid.shape[-1]
    me_s = lax.axis_index("dp")
    me_v = lax.axis_index("vocab")
    y, zl = me_s // 2, me_s % 2
    x, c = me_v // (2 * nzh), me_v % 2
    xp = x % 2
    other = 2 * y + 1 - zl
    y_nbr = [{"dp": ((y + 1) % ny) * 2 + zl}, {"dp": ((y + ny - 1) % ny) * 2 + zl}]
    x_nbr = [
        {"vocab": ((x + 1) % nx) * (2 * nzh) + me_v % (2 * nzh)},
        {"vocab": ((x + nx - 1) % nx) * (2 * nzh) + me_v % (2 * nzh)},
    ]
    sib = {"vocab": me_v + 1 - 2 * c}
    z_peer = {"dp": other}
    base = xp * 64 + c * 32
    obase = (1 - xp) * 64 + c * 32
    base_sib = xp * 64 + (1 - c) * 32
    obase_sib = (1 - xp) * 64 + (1 - c) * 32

    def rows(start, count):
        return pl.ds(pl.multiple_of(start, 16), count)

    def reg2(yb, start, count):
        return hid.at[pl.ds(2 * yb, 2), rows(start, count), :]

    def reg1(s, start, count):
        return hid.at[s, rows(start, count), :]

    def wait(ref, sem):
        pltpu.make_async_copy(ref, ref, sem).wait()

    sent = []

    def send(src, dst, ssem, rsem, dev):
        copy = pltpu.make_async_remote_copy(
            src_ref=src, dst_ref=dst, send_sem=ssem, recv_sem=rsem,
            device_id=dev, device_id_type=MESH,
        )
        copy.start()
        sent.append((src, ssem))

    def send_quiet(src, dst, ssem, rsem, dev):
        pltpu.make_async_remote_copy(
            src_ref=src, dst_ref=dst, send_sem=ssem, recv_sem=rsem,
            device_id=dev, device_id_type=MESH,
        ).start()

    own = pltpu.make_async_copy(hidden_ref, hid.at[me_s], loc.at[0])
    own.start()
    tload = pltpu.make_async_copy(teacher_hbm, tv, loc.at[1])
    tload.start()
    hload = pltpu.make_async_copy(head_hbm, head, loc.at[2])
    hload.start()

    barrier = pltpu.get_barrier_semaphore()

    def greet_dp(i, _):
        pl.semaphore_signal(
            barrier, inc=1, device_id={"dp": (me_s + i) % n_dp}, device_id_type=MESH
        )
        return 0

    def greet_v(i, _):
        pl.semaphore_signal(
            barrier, inc=1, device_id={"vocab": (me_v + i) % n_v}, device_id_type=MESH
        )
        return 0

    lax.fori_loop(1, n_dp, greet_dp, 0)
    lax.fori_loop(1, n_v, greet_v, 0)
    pl.semaphore_wait(barrier, n_dp + n_v - 2)

    send(hidden_ref.at[rows(base, 32), :], reg1(me_s, base, 32), zs.at[0], zr.at[0], z_peer)

    def first_rows(g):
        return (base, 32) if half > 1 else (base + 16 * g, 16)

    for g in range(2):
        st, ct = first_rows(g)
        send(hidden_ref.at[rows(st, ct), :], reg1(me_s, st, ct),
             ys.at[g, 0], yr.at[g, 0], y_nbr[g])

    tload.wait()

    def t1_step(i, _):
        s = (me_s + i) % n_dp
        cols = pl.ds(pl.multiple_of(s * SUB, SUB), SUB)
        block = jnp.transpose(tv[:, cols])
        tt[2 * s] = block[:128]
        tt[2 * s + 1] = block[128:]
        send_quiet(tt.at[pl.ds(2 * s, 2)], rr.at[pl.ds(2 * me_s, 2)],
                   t1s.at[0], t1r.at[me_s], {"dp": s})
        return 0

    lax.fori_loop(1, n_dp, t1_step, 0)
    own_block = jnp.transpose(tv[:, pl.ds(pl.multiple_of(me_s * SUB, SUB), SUB)])
    tt[2 * me_s] = own_block[:128]
    tt[2 * me_s + 1] = own_block[128:]
    rr[2 * me_s] = own_block[:128]
    rr[2 * me_s + 1] = own_block[128:]

    def t2_step(s):
        for h in range(2):
            k = 2 * s + h

            @pl.when(k != me_v)
            def _():
                send_quiet(rr.at[k], qq.at[me_v], t2s.at[0], t2r.at[0], {"vocab": k})

            @pl.when(k == me_v)
            def _():
                qq[me_v] = rr[k]

    def t2_range(lo, hi):
        def body(i, _):
            s = (me_s + n_dp - i) % n_dp
            wait(rr.at[pl.ds(2 * s, 2)], t1r.at[s])
            t2_step(s)
            return 0

        lax.fori_loop(lo, hi, body, 0)

    def t3_all():
        wait(qq.at[pl.ds(0, n_v - 1)], t2r.at[0])

        def body(j, _):
            v = (me_v + j) % n_v
            ww[v] = qq[inv_ref[v]]
            send_quiet(ww.at[v], tgt.at[me_v], t3s.at[0], t3r.at[0], {"vocab": v})
            return 0

        lax.fori_loop(1, n_v, body, 0)
        tgt[me_v] = qq[inv_ref[me_v]]

    row_id = lax.broadcasted_iota(jnp.int32, (8, 128), 0)

    def as_tile(parts):
        tile = jnp.zeros((8, 128), F32)
        for r, part in enumerate(parts):
            tile = jnp.where(row_id == r, part, tile)
        return tile

    def teacher_stats():
        def mx(i, acc):
            return jnp.maximum(acc, tt[i].astype(F32))

        top = lax.fori_loop(1, n_v, mx, tt[0].astype(F32))
        top = jnp.max(top, axis=0, keepdims=True)

        def sm(i, acc):
            return acc + jnp.exp(tt[i].astype(F32) - top)

        total = lax.fori_loop(0, n_v, sm, jnp.zeros((128, 128), F32))
        total = jnp.sum(total, axis=0, keepdims=True)
        tst[...] = as_tile([top, total])

    def block_y(idx):
        d = (idx + 1) // 2
        return (y + ny - d) % ny if idx % 2 == 1 else (y + d) % ny

    def send_x(idx, q):
        yb = block_y(idx)
        part = reg1(other, base + 16 * q, 16) if idx == 0 else reg2(yb, base + 16 * q, 16)
        send(part, part, xs.at[q, idx], xr.at[q, idx], x_nbr[q])

    def send_core(idx, kind):
        yb = block_y(idx)
        st = base if kind == 0 else obase
        part = reg1(other, st, 32) if idx == 0 else reg2(yb, st, 32)
        send(part, part, cs.at[kind, idx], cr.at[kind, idx], sib)

    def y_recv(idx):
        yb = block_y(idx)
        d = (idx + 1) // 2
        if idx == 0:
            wait(reg1(other, base, 32), zr.at[0])
            for g in range(2):
                st, ct = first_rows(g)
                part = reg1(other, st, ct)
                send(part, part, ys.at[g, 1], yr.at[g, 1], y_nbr[g])
            for q in range(2):
                send_x(idx, q)
        elif d < half:
            g = 0 if idx % 2 == 1 else 1
            if d == 1:
                wait(reg1(2 * yb + zl, base, 32), yr.at[g, 0])
                wait(reg1(2 * yb + 1 - zl, base, 32), yr.at[g, 1])
            for q in ((0, 1) if g == 0 else (1, 0)):
                if d > 1:
                    wait(reg2(yb, base + 16 * q, 16), yr.at[g, 2 * (d - 1) + q])
                if d + 1 < half or q == g:
                    part = reg2(yb, base + 16 * q, 16)
                    send(part, part, ys.at[g, 2 * d + q], yr.at[g, 2 * d + q], y_nbr[g])
                send_x(idx, q)
        else:
            for g in range(2):
                if d == 1:
                    wait(reg1(2 * yb + zl, base + 16 * g, 16), yr.at[g, 0])
                    wait(reg1(2 * yb + 1 - zl, base + 16 * g, 16), yr.at[g, 1])
                else:
                    wait(reg2(yb, base + 16 * g, 16), yr.at[g, 2 * (d - 1) + g])
                send_x(idx, g)
        send_core(idx, 0)

    def x_recv(idx):
        yb = block_y(idx)
        for q in range(2):
            part = reg1(other, obase + 16 * q, 16) if idx == 0 else reg2(yb, obase + 16 * q, 16)
            wait(part, xr.at[q, idx])
        send_core(idx, 1)

    def compute(idx):
        yb = block_y(idx)
        for kind in range(2):
            st = base_sib if kind == 0 else obase_sib
            part = reg1(other, st, 32) if idx == 0 else reg2(yb, st, 32)
            wait(part, cr.at[kind, idx])
        block = hid[pl.ds(2 * yb, 2)].reshape(256, d_model)
        scores = lax.dot_general(
            head[...], block, (((1,), (1,)), ((), ())), preferred_element_type=F32
        )
        cols = pl.ds(pl.multiple_of(yb * 256, 256), 256)
        sc[:, cols] = scores
        top = jnp.max(scores, axis=0, keepdims=True)
        e = jnp.exp(scores - top)
        ex[:, cols] = e
        total = jnp.sum(e, axis=0, keepdims=True)
        for j in range(2):
            lanes = slice(128 * j, 128 * j + 128)
            src1[2 * yb + j] = as_tile([top[:, lanes], total[:, lanes]])

    own.wait()
    hload.wait()
    t2_step(me_s)
    t2_plan = {1: (1, 3), 2: (3, 7), 3: (7, 12), 4: (12, n_dp)}
    t3_stage = 6
    t2_done, t3_done = 1, False
    for stage in range(ny + 2):
        if stage < ny:
            y_recv(stage)
        if stage == 0:
            teacher_stats()
        if stage in t2_plan:
            lo, hi = t2_plan[stage]
            lo, hi = min(lo, n_dp), min(hi, n_dp)
            if hi > lo:
                t2_range(lo, hi)
            t2_done = hi
        if 1 <= stage <= ny:
            x_recv(stage - 1)
        if stage >= 2:
            compute(stage - 2)
        if stage == t3_stage:
            t3_all()
            t3_done = True
    if t2_done < n_dp:
        t2_range(t2_done, n_dp)
    if not t3_done:
        t3_all()

    def spread_dp(src, dst, k):
        def body(i, _):
            s = (me_s + i) % n_dp
            send_quiet(src.at[s], dst.at[me_s], as_.at[k], ar_.at[k], {"dp": s})
            return 0

        lax.fori_loop(1, n_dp, body, 0)
        dst[me_s] = src[me_s]

    def share_v(tile, dst, k):
        def body(i, _):
            send_quiet(tile, dst.at[me_v], as_.at[k], ar_.at[k], {"vocab": (me_v + i) % n_v})
            return 0

        lax.fori_loop(1, n_v, body, 0)
        dst[me_v] = tile[...]

    def share_dp(tile, dst, k):
        def body(i, _):
            send_quiet(tile, dst.at[me_s], as_.at[k], ar_.at[k], {"dp": (me_s + i) % n_dp})
            return 0

        lax.fori_loop(1, n_dp, body, 0)
        dst[me_s] = tile[...]

    def merge(ref, r):
        tops = ref[:, r, :]
        sums = ref[:, r + 1, :]
        top = jnp.max(tops, axis=0, keepdims=True)
        return top, jnp.sum(sums * jnp.exp(tops - top), axis=0, keepdims=True)

    spread_dp(src1, ar1, 0)
    wait(ar1.at[pl.ds(0, n_dp - 1)], ar_.at[0])
    top, total = merge(ar1, 0)
    tile2[...] = as_tile([top, total, tst[0:1, :], tst[1:2, :]])
    share_v(tile2, ar2, 1)
    wait(ar2.at[pl.ds(0, n_v - 1)], ar_.at[1])
    top, total = merge(ar2, 0)
    t_top, t_total = merge(ar2, 2)
    tile3[...] = as_tile([top, total, t_top, t_total])
    share_dp(tile3, fin, 2)
    wait(fin.at[pl.ds(0, n_dp - 1)], ar_.at[2])

    wait(tgt.at[pl.ds(0, n_v - 1)], t3r.at[0])

    def grad_chunk(s, _):
        cols = pl.ds(pl.multiple_of(s * 128, 128), 128)
        f = fin[s]
        m_s, z_s, m_t, z_t = f[0:1], f[1:2], f[2:3], f[3:4]
        w = weight_ref[s]
        scale_s = w * jnp.exp(src1[s][0:1] - m_s) / z_s
        scale_t = w / z_t
        cross = jnp.zeros((1, 128), F32)
        for h in range(2):
            t = tgt[2 * s + h].astype(F32)
            e_t = jnp.exp(t - m_t)
            band = slice(128 * h, 128 * h + 128)
            cross = cross + jnp.sum(e_t * (t - sc[band, cols]), axis=0, keepdims=True)
            pr[band, cols] = (ex[band, cols] * scale_s - e_t * scale_t).astype(BF16)
        csrc1[s] = as_tile([cross])
        return 0

    lax.fori_loop(0, n_dp, grad_chunk, 0)

    n_tiles = d_model // 256

    def gemm(lo, hi):
        def body(n, _):
            cols = pl.ds(pl.multiple_of(n * 256, 256), 256)
            b = hid[:, :, cols].reshape(n_dp * 128, 256)
            grad_ref[:, cols] = jnp.dot(pr[...], b, preferred_element_type=F32).astype(BF16)
            return 0

        lax.fori_loop(lo, hi, body, 0)

    cut1, cut2 = n_tiles // 3, 2 * n_tiles // 3
    spread_dp(csrc1, car1, 3)
    gemm(0, cut1)
    wait(car1.at[pl.ds(0, n_dp - 1)], ar_.at[3])
    ctile2[...] = jnp.sum(car1[...], axis=0)
    share_v(ctile2, car2, 4)
    gemm(cut1, cut2)
    wait(car2.at[pl.ds(0, n_v - 1)], ar_.at[4])
    ctile3[...] = jnp.sum(car2[...], axis=0)
    share_dp(ctile3, cfin, 5)
    gemm(cut2, n_tiles)
    wait(cfin.at[pl.ds(0, n_dp - 1)], ar_.at[5])
    m_s, z_s, m_t, z_t = fin[:, 0, :], fin[:, 1, :], fin[:, 2, :], fin[:, 3, :]
    div_ref[...] = cfin[:, 0, :] / z_t - m_t - jnp.log(z_t) + m_s + jnp.log(z_s)

    for ref, sem in sent:
        wait(ref, sem)
    wait(tt.at[pl.ds(0, 2 * (n_dp - 1))], t1s.at[0])
    wait(rr.at[pl.ds(0, n_v - 1)], t2s.at[0])
    wait(ww.at[pl.ds(0, n_v - 1)], t3s.at[0])
    for k, ref in ((0, ar1), (1, ar2), (2, fin), (3, car1), (4, car2), (5, cfin)):
        wait(ref.at[pl.ds(0, (n_v if k % 3 == 1 else n_dp) - 1)], as_.at[k])


def on_device(nx, ny, nzh, hidden, head, teacher, shard_order, loss_weight):
    n_dp, n_v = 2 * ny, 2 * nx * nzh
    d_model = hidden.shape[1]
    tokens = n_dp * 128
    ordinal = jnp.arange(n_v, dtype=jnp.int32)
    matches = (shard_order[None, :] == ordinal[:, None]).astype(jnp.int32)
    inverse = jnp.sum(matches * ordinal[None, :], axis=1)
    any_ = pl.BlockSpec(memory_space=pl.ANY)
    vmem = pl.BlockSpec(memory_space=pltpu.VMEM)
    smem = pl.BlockSpec(memory_space=pltpu.SMEM)
    dma = pltpu.SemaphoreType.DMA

    def stat(n):
        return pltpu.VMEM((n, 8, 128), F32)

    tile = pltpu.VMEM((8, 128), F32)
    pieces = pltpu.VMEM((n_v, 128, 128), BF16)
    grad, div = pl.pallas_call(
        functools.partial(kernel, nx, ny, nzh),
        out_shape=(
            jax.ShapeDtypeStruct((SUB, d_model), BF16),
            jax.ShapeDtypeStruct((n_dp, 128), F32),
        ),
        in_specs=[smem, any_, any_, any_, vmem],
        out_specs=(vmem, vmem),
        scratch_shapes=[
            pltpu.VMEM((n_dp, 128, d_model), BF16),
            pltpu.VMEM((SUB, d_model), BF16),
            pltpu.VMEM((128, n_dp * SUB), BF16),
            pieces, pieces, pieces, pieces, pieces,
            pltpu.VMEM((SUB, tokens), F32),
            pltpu.VMEM((SUB, tokens), F32),
            pltpu.VMEM((SUB, tokens), BF16),
            stat(n_dp), stat(n_dp), tile, stat(n_v), tile, stat(n_dp), tile,
            stat(n_dp), stat(n_dp), tile, stat(n_v), tile, stat(n_dp),
            dma((3,)),
            dma((1,)), dma((1,)),
            dma((2, ny)), dma((2, ny)),
            dma((2, ny)), dma((2, ny)),
            dma((2, ny)), dma((2, ny)),
            dma((1,)), dma((n_dp,)),
            dma((1,)), dma((1,)),
            dma((1,)), dma((1,)),
            dma((6,)), dma((6,)),
        ],
        compiler_params=pltpu.CompilerParams(
            collective_id=0, has_side_effects=True, vmem_limit_bytes=56 * 1024 * 1024
        ),
        cost_estimate=pl.CostEstimate(
            flops=4 * SUB * tokens * d_model, bytes_accessed=8 * SUB * d_model, transcendentals=0
        ),
    )(inverse, hidden, head[0], teacher, loss_weight.reshape(n_dp, 1, 128))
    return grad[None], div.reshape(tokens)


def build(mesh, nx, ny, nzh):
    in_specs = (P("dp", None), P("dp", "vocab", None), P("dp", "vocab"), P(), P())
    out_specs = (P("dp", "vocab", None), P())
    return jax.shard_map(
        functools.partial(on_device, nx, ny, nzh),
        mesh=mesh, in_specs=in_specs, out_specs=out_specs, check_vma=False,
    )


def solution(mesh):
    return build(mesh, 4, mesh.shape["dp"] // 2, mesh.shape["vocab"] // 8)
```

```python
import functools

import jax
import jax.numpy as jnp
from jax import lax
from jax.experimental import pallas as pl
from jax.experimental.pallas import tpu as pltpu
from jax.sharding import PartitionSpec as P

F32 = jnp.float32
BF16 = jnp.bfloat16
MESH = pl.DeviceIdType.MESH
SUB = 256


def kernel(
    nx, ny, nzh,
    order_ref, hidden_ref, head_hbm, teacher_hbm, weight_ref,
    grad_ref, div_ref,
    inv, hid, head, tv, tt, rr, qq, ww, tgt, sc, ex, pr,
    src1, ar1, tile2, ar2, tile3, fin,
    csrc1, car1, ctile2, car2, ctile3, cfin,
    loc, zs, zr, ys, yr, xs, xr, cs, cr, t1s, t1r, t2s, t2r, t3s, t3r, as_, ar_,
):
    half = ny // 2
    n_dp = 2 * ny
    n_v = 2 * nx * nzh
    d_model = hid.shape[-1]
    me_s = lax.axis_index("dp")
    me_v = lax.axis_index("vocab")
    y, zl = me_s // 2, me_s % 2
    x, c = me_v // (2 * nzh), me_v % 2
    xp = x % 2
    other = 2 * y + 1 - zl
    y_nbr = [{"dp": ((y + 1) % ny) * 2 + zl}, {"dp": ((y + ny - 1) % ny) * 2 + zl}]
    x_nbr = [
        {"vocab": ((x + 1) % nx) * (2 * nzh) + me_v % (2 * nzh)},
        {"vocab": ((x + nx - 1) % nx) * (2 * nzh) + me_v % (2 * nzh)},
    ]
    sib = {"vocab": me_v + 1 - 2 * c}
    z_peer = {"dp": other}
    base = xp * 64 + c * 32
    obase = (1 - xp) * 64 + c * 32
    base_sib = xp * 64 + (1 - c) * 32
    obase_sib = (1 - xp) * 64 + (1 - c) * 32

    def rows(start, count):
        return pl.ds(pl.multiple_of(start, 16), count)

    def reg2(yb, start, count):
        return hid.at[pl.ds(2 * yb, 2), rows(start, count), :]

    def reg1(s, start, count):
        return hid.at[s, rows(start, count), :]

    def wait(ref, sem):
        pltpu.make_async_copy(ref, ref, sem).wait()

    sent = []

    def send(src, dst, ssem, rsem, dev):
        copy = pltpu.make_async_remote_copy(
            src_ref=src, dst_ref=dst, send_sem=ssem, recv_sem=rsem,
            device_id=dev, device_id_type=MESH,
        )
        copy.start()
        sent.append((src, ssem))

    def send_quiet(src, dst, ssem, rsem, dev):
        pltpu.make_async_remote_copy(
            src_ref=src, dst_ref=dst, send_sem=ssem, recv_sem=rsem,
            device_id=dev, device_id_type=MESH,
        ).start()

    own = pltpu.make_async_copy(hidden_ref, hid.at[me_s], loc.at[0])
    own.start()
    tload = pltpu.make_async_copy(teacher_hbm, tv, loc.at[1])
    tload.start()
    hload = pltpu.make_async_copy(head_hbm, head, loc.at[2])
    hload.start()

    barrier = pltpu.get_barrier_semaphore()

    def greet_dp(i, _):
        pl.semaphore_signal(
            barrier, inc=1, device_id={"dp": (me_s + i) % n_dp}, device_id_type=MESH
        )
        return 0

    def greet_v(i, _):
        pl.semaphore_signal(
            barrier, inc=1, device_id={"vocab": (me_v + i) % n_v}, device_id_type=MESH
        )
        return 0

    lax.fori_loop(1, n_dp, greet_dp, 0)
    lax.fori_loop(1, n_v, greet_v, 0)
    tload.wait()

    def flip(k, _):
        tt[k] = jnp.transpose(tv[:, pl.ds(pl.multiple_of(k * 128, 128), 128)])
        return 0

    lax.fori_loop(0, n_v, flip, 0)
    pl.semaphore_wait(barrier, n_dp + n_v - 2)

    send(hidden_ref.at[rows(base, 32), :], reg1(me_s, base, 32), zs.at[0], zr.at[0], z_peer)

    def first_rows(g):
        return (base, 32) if half > 1 else (base + 16 * g, 16)

    for g in range(2):
        st, ct = first_rows(g)
        send(hidden_ref.at[rows(st, ct), :], reg1(me_s, st, ct),
             ys.at[g, 0], yr.at[g, 0], y_nbr[g])

    def t2_step(j, _):
        k = (me_v + j) % n_v
        send_quiet(tt.at[k], qq.at[me_v], t2s.at[0], t2r.at[0], {"vocab": k})
        return 0

    lax.fori_loop(1, n_v, t2_step, 0)
    qq[me_v] = tt[me_v]

    def inverse_of(v, _):
        found = order_ref[0] * 0
        for b in range(n_v):
            found = jnp.maximum(found, jnp.where(order_ref[b] == v, b, 0))
        inv[v] = found
        return 0

    lax.fori_loop(0, n_v, inverse_of, 0)
    my_pair = me_v // 2

    def t3_all():
        wait(qq.at[pl.ds(0, n_v - 1)], t2r.at[0])

        def body(j, _):
            vp = (j + me_s + n_dp - my_pair) % n_dp
            for cc in range(2):
                v = 2 * vp + cc

                @pl.when(v != me_v)
                def _():
                    ww[v] = qq[inv[v]]
                    send_quiet(ww.at[v], rr.at[me_v], t3s.at[0], t3r.at[me_v], {"vocab": v})

                @pl.when(v == me_v)
                def _():
                    rr[v] = qq[inv[v]]

            return 0

        lax.fori_loop(0, n_dp, body, 0)

    def t1_range(lo, hi):
        def body(j, _):
            s = (j + me_s + n_dp - my_pair) % n_dp
            for cc in range(2):
                k = 2 * s + cc

                @pl.when(k != me_v)
                def _():
                    wait(rr.at[k], t3r.at[k])

            @pl.when(s != me_s)
            def _():
                send_quiet(rr.at[pl.ds(2 * s, 2)], tgt.at[pl.ds(2 * me_s, 2)],
                           t1s.at[0], t1r.at[0], {"dp": s})

            @pl.when(s == me_s)
            def _():
                tgt[2 * s] = rr[2 * s]
                tgt[2 * s + 1] = rr[2 * s + 1]

            return 0

        lax.fori_loop(lo, hi, body, 0)

    def teacher_stats():
        def mx(i, acc):
            return jnp.maximum(acc, tt[i].astype(F32))

        top = lax.fori_loop(1, n_v, mx, tt[0].astype(F32))
        top = jnp.max(top, axis=0, keepdims=True)

        def sm(i, acc):
            return acc + jnp.exp(tt[i].astype(F32) - top)

        total = lax.fori_loop(0, n_v, sm, jnp.zeros((128, 128), F32))
        tile2[2:3, :] = top
        tile2[3:4, :] = jnp.sum(total, axis=0, keepdims=True)

    def block_y(idx):
        d = (idx + 1) // 2
        return (y + ny - d) % ny if idx % 2 == 1 else (y + d) % ny

    def send_x(idx, q):
        yb = block_y(idx)
        part = reg1(other, base + 16 * q, 16) if idx == 0 else reg2(yb, base + 16 * q, 16)
        send(part, part, xs.at[q, idx], xr.at[q, idx], x_nbr[q])

    def send_core(idx, kind):
        yb = block_y(idx)
        st = base if kind == 0 else obase
        part = reg1(other, st, 32) if idx == 0 else reg2(yb, st, 32)
        send(part, part, cs.at[kind, idx], cr.at[kind, idx], sib)

    def y_recv(idx):
        yb = block_y(idx)
        d = (idx + 1) // 2
        if idx == 0:
            wait(reg1(other, base, 32), zr.at[0])
            for g in range(2):
                st, ct = first_rows(g)
                part = reg1(other, st, ct)
                send(part, part, ys.at[g, 1], yr.at[g, 1], y_nbr[g])
            for q in range(2):
                send_x(idx, q)
        elif d < half:
            g = 0 if idx % 2 == 1 else 1
            if d == 1:
                wait(reg1(2 * yb + zl, base, 32), yr.at[g, 0])
                wait(reg1(2 * yb + 1 - zl, base, 32), yr.at[g, 1])
            for q in ((0, 1) if g == 0 else (1, 0)):
                if d > 1:
                    wait(reg2(yb, base + 16 * q, 16), yr.at[g, 2 * (d - 1) + q])
                if d + 1 < half or q == g:
                    part = reg2(yb, base + 16 * q, 16)
                    send(part, part, ys.at[g, 2 * d + q], yr.at[g, 2 * d + q], y_nbr[g])
                send_x(idx, q)
        else:
            for g in range(2):
                if d == 1:
                    wait(reg1(2 * yb + zl, base + 16 * g, 16), yr.at[g, 0])
                    wait(reg1(2 * yb + 1 - zl, base + 16 * g, 16), yr.at[g, 1])
                else:
                    wait(reg2(yb, base + 16 * g, 16), yr.at[g, 2 * (d - 1) + g])
                send_x(idx, g)
        send_core(idx, 0)

    def x_recv(idx):
        yb = block_y(idx)
        for q in range(2):
            part = reg1(other, obase + 16 * q, 16) if idx == 0 else reg2(yb, obase + 16 * q, 16)
            wait(part, xr.at[q, idx])
        send_core(idx, 1)

    def compute(idx):
        yb = block_y(idx)
        for kind in range(2):
            st = base_sib if kind == 0 else obase_sib
            part = reg1(other, st, 32) if idx == 0 else reg2(yb, st, 32)
            wait(part, cr.at[kind, idx])
        block = hid[pl.ds(2 * yb, 2)].reshape(256, d_model)
        scores = lax.dot_general(
            head[...], block, (((1,), (1,)), ((), ())), preferred_element_type=F32
        )
        cols = pl.ds(pl.multiple_of(yb * 256, 256), 256)
        sc[:, cols] = scores
        top = jnp.max(scores, axis=0, keepdims=True)
        e = jnp.exp(scores - top)
        ex[:, cols] = e
        total = jnp.sum(e, axis=0, keepdims=True)
        for j in range(2):
            lanes = slice(128 * j, 128 * j + 128)
            src1[2 * yb + j, 0:1, :] = top[:, lanes]
            src1[2 * yb + j, 1:2, :] = total[:, lanes]

    own.wait()
    hload.wait()
    t1_plan = {ny - 1: (0, 3), ny: (3, 6), ny + 1: (6, 9)}
    for stage in range(ny + 2):
        if stage < ny:
            y_recv(stage)
        if stage == 0:
            teacher_stats()
        if 1 <= stage <= ny:
            x_recv(stage - 1)
        if stage >= 2:
            compute(stage - 2)
        if stage == max(ny - 2, 0):
            t3_all()
        if stage in t1_plan:
            lo, hi = t1_plan[stage]
            t1_range(min(lo, n_dp), min(hi, n_dp))

    def spread_dp(src, dst, k):
        def body(i, _):
            s = (me_s + i) % n_dp
            send_quiet(src.at[s], dst.at[me_s], as_.at[k], ar_.at[k], {"dp": s})
            return 0

        lax.fori_loop(1, n_dp, body, 0)
        dst[me_s] = src[me_s]

    def share_v(tile, dst, k):
        def body(i, _):
            send_quiet(tile, dst.at[me_v], as_.at[k], ar_.at[k], {"vocab": (me_v + i) % n_v})
            return 0

        lax.fori_loop(1, n_v, body, 0)
        dst[me_v] = tile[...]

    def share_dp(tile, dst, k):
        def body(i, _):
            send_quiet(tile, dst.at[me_s], as_.at[k], ar_.at[k], {"dp": (me_s + i) % n_dp})
            return 0

        lax.fori_loop(1, n_dp, body, 0)
        dst[me_s] = tile[...]

    def merge(ref, r):
        tops = ref[:, r, :]
        sums = ref[:, r + 1, :]
        top = jnp.max(tops, axis=0, keepdims=True)
        return top, jnp.sum(sums * jnp.exp(tops - top), axis=0, keepdims=True)

    spread_dp(src1, ar1, 0)
    t1_range(min(9, n_dp), min(12, n_dp))
    wait(ar1.at[pl.ds(0, n_dp - 1)], ar_.at[0])
    tile2[0:1, :], tile2[1:2, :] = merge(ar1, 0)
    share_v(tile2, ar2, 1)
    t1_range(min(12, n_dp), n_dp)
    wait(ar2.at[pl.ds(0, n_v - 1)], ar_.at[1])
    tile3[0:1, :], tile3[1:2, :] = merge(ar2, 0)
    tile3[2:3, :], tile3[3:4, :] = merge(ar2, 2)
    share_dp(tile3, fin, 2)
    wait(fin.at[pl.ds(0, n_dp - 1)], ar_.at[2])

    wait(tgt.at[pl.ds(0, n_v - 2)], t1r.at[0])

    def grad_chunk(s, _):
        cols = pl.ds(pl.multiple_of(s * 128, 128), 128)
        f = fin[s]
        m_s, z_s, m_t, z_t = f[0:1], f[1:2], f[2:3], f[3:4]
        w = weight_ref[s]
        scale_s = w * jnp.exp(src1[s][0:1] - m_s) / z_s
        scale_t = w / z_t
        cross = jnp.zeros((1, 128), F32)
        for h in range(2):
            t = tgt[2 * s + h].astype(F32)
            e_t = jnp.exp(t - m_t)
            band = slice(128 * h, 128 * h + 128)
            cross = cross + jnp.sum(e_t * (t - sc[band, cols]), axis=0, keepdims=True)
            pr[band, cols] = (ex[band, cols] * scale_s - e_t * scale_t).astype(BF16)
        csrc1[s] = cross
        return 0

    lax.fori_loop(0, n_dp, grad_chunk, 0)

    n_tiles = d_model // 256

    def gemm(lo, hi):
        def body(n, _):
            cols = pl.ds(pl.multiple_of(n * 256, 256), 256)
            b = hid[:, :, cols].reshape(n_dp * 128, 256)
            grad_ref[:, cols] = jnp.dot(pr[...], b, preferred_element_type=F32).astype(BF16)
            return 0

        lax.fori_loop(lo, hi, body, 0)

    cut1, cut2 = n_tiles // 3, 2 * n_tiles // 3
    spread_dp(csrc1, car1, 3)
    gemm(0, cut1)
    wait(car1.at[pl.ds(0, n_dp - 1)], ar_.at[3])
    ctile2[...] = jnp.sum(car1[...], axis=0)
    share_v(ctile2, car2, 4)
    gemm(cut1, cut2)
    wait(car2.at[pl.ds(0, n_v - 1)], ar_.at[4])
    ctile3[...] = jnp.sum(car2[...], axis=0)
    share_dp(ctile3, cfin, 5)
    gemm(cut2, n_tiles)
    wait(cfin.at[pl.ds(0, n_dp - 1)], ar_.at[5])
    m_s, z_s, m_t, z_t = fin[:, 0, :], fin[:, 1, :], fin[:, 2, :], fin[:, 3, :]
    div_ref[...] = cfin[:, 0, :] / z_t - m_t - jnp.log(z_t) + m_s + jnp.log(z_s)

    for ref, sem in sent:
        wait(ref, sem)
    wait(tt.at[pl.ds(0, n_v - 1)], t2s.at[0])
    wait(rr.at[pl.ds(0, n_v - 2)], t1s.at[0])
    wait(ww.at[pl.ds(0, n_v - 1)], t3s.at[0])
    for k, ref in ((0, ar1), (1, ar2), (2, fin), (3, car1), (4, car2), (5, cfin)):
        wait(ref.at[pl.ds(0, (n_v if k % 3 == 1 else n_dp) - 1)], as_.at[k])


def on_device(nx, ny, nzh, hidden, head, teacher, shard_order, loss_weight):
    n_dp, n_v = 2 * ny, 2 * nx * nzh
    d_model = hidden.shape[1]
    tokens = n_dp * 128
    any_ = pl.BlockSpec(memory_space=pl.ANY)
    vmem = pl.BlockSpec(memory_space=pltpu.VMEM)
    smem = pl.BlockSpec(memory_space=pltpu.SMEM)
    dma = pltpu.SemaphoreType.DMA

    def stat(n, r):
        return pltpu.VMEM((n, r, 128), F32)

    tile4, tile1 = pltpu.VMEM((4, 128), F32), pltpu.VMEM((1, 128), F32)
    pieces = pltpu.VMEM((n_v, 128, 128), BF16)
    grad, div = pl.pallas_call(
        functools.partial(kernel, nx, ny, nzh),
        out_shape=(
            jax.ShapeDtypeStruct((SUB, d_model), BF16),
            jax.ShapeDtypeStruct((n_dp, 128), F32),
        ),
        in_specs=[smem, any_, any_, any_, vmem],
        out_specs=(vmem, vmem),
        scratch_shapes=[
            pltpu.SMEM((n_v,), jnp.int32),
            pltpu.VMEM((n_dp, 128, d_model), BF16),
            pltpu.VMEM((SUB, d_model), BF16),
            pltpu.VMEM((128, n_dp * SUB), BF16),
            pieces, pieces, pieces, pieces, pieces,
            pltpu.VMEM((SUB, tokens), F32),
            pltpu.VMEM((SUB, tokens), F32),
            pltpu.VMEM((SUB, tokens), BF16),
            stat(n_dp, 2), stat(n_dp, 2), tile4, stat(n_v, 4), tile4, stat(n_dp, 4),
            stat(n_dp, 1), stat(n_dp, 1), tile1, stat(n_v, 1), tile1, stat(n_dp, 1),
            dma((3,)),
            dma((1,)), dma((1,)),
            dma((2, ny)), dma((2, ny)),
            dma((2, ny)), dma((2, ny)),
            dma((2, ny)), dma((2, ny)),
            dma((1,)), dma((1,)),
            dma((1,)), dma((1,)),
            dma((1,)), dma((n_v,)),
            dma((6,)), dma((6,)),
        ],
        compiler_params=pltpu.CompilerParams(
            collective_id=0, has_side_effects=True, vmem_limit_bytes=56 * 1024 * 1024
        ),
        cost_estimate=pl.CostEstimate(
            flops=4 * SUB * tokens * d_model, bytes_accessed=8 * SUB * d_model, transcendentals=0
        ),
    )(shard_order, hidden, head[0], teacher, loss_weight.reshape(n_dp, 1, 128))
    return grad[None], div.reshape(tokens)


def build(mesh, nx, ny, nzh):
    in_specs = (P("dp", None), P("dp", "vocab", None), P("dp", "vocab"), P(), P())
    out_specs = (P("dp", "vocab", None), P())
    return jax.shard_map(
        functools.partial(on_device, nx, ny, nzh),
        mesh=mesh, in_specs=in_specs, out_specs=out_specs, check_vma=False,
    )


def solution(mesh):
    return build(mesh, 4, mesh.shape["dp"] // 2, mesh.shape["vocab"] // 8)
```

```python
import functools

import jax
import jax.numpy as jnp
from jax import lax
from jax.experimental import pallas as pl
from jax.experimental.pallas import tpu as pltpu
from jax.sharding import PartitionSpec as P

F32 = jnp.float32
BF16 = jnp.bfloat16
MESH = pl.DeviceIdType.MESH
SUB = 256


def kernel(
    nx, ny, nzh,
    order_ref, hidden_ref, head_hbm, teacher_hbm, weight_ref,
    grad_ref, div_ref,
    inv, hid, head, tv, tt, picked, qq, ww, tgt, sc, ex, pr,
    src1, ar1, tile2, ar2, tile3, fin,
    csrc1, car1, ctile2, car2, ctile3, cfin,
    loc, zs, zr, ys, yr, xs, xr, cs, cr, t2s, t2r, t3s, t3r, as_, ar_,
):
    half = ny // 2
    n_dp = 2 * ny
    n_v = 2 * nx * nzh
    d_model = hid.shape[-1]
    me_s = lax.axis_index("dp")
    me_v = lax.axis_index("vocab")
    y, zl = me_s // 2, me_s % 2
    x, zh, c = me_v // (2 * nzh), (me_v // 2) % nzh, me_v % 2
    xp = x % 2
    other = 2 * y + 1 - zl
    y_nbr = [{"dp": ((y + 1) % ny) * 2 + zl}, {"dp": ((y + ny - 1) % ny) * 2 + zl}]
    x_nbr = [
        {"vocab": ((x + 1) % nx) * (2 * nzh) + me_v % (2 * nzh)},
        {"vocab": ((x + nx - 1) % nx) * (2 * nzh) + me_v % (2 * nzh)},
    ]
    sib = {"vocab": me_v + 1 - 2 * c}
    z_peer = {"dp": other}
    base = xp * 64 + c * 32
    obase = (1 - xp) * 64 + c * 32
    base_sib = xp * 64 + (1 - c) * 32
    obase_sib = (1 - xp) * 64 + (1 - c) * 32

    def rows(start, count):
        return pl.ds(pl.multiple_of(start, 16), count)

    def reg2(yb, start, count):
        return hid.at[pl.ds(2 * yb, 2), rows(start, count), :]

    def reg1(s, start, count):
        return hid.at[s, rows(start, count), :]

    def wait(ref, sem):
        pltpu.make_async_copy(ref, ref, sem).wait()

    sent = []

    def send(src, dst, ssem, rsem, dev):
        copy = pltpu.make_async_remote_copy(
            src_ref=src, dst_ref=dst, send_sem=ssem, recv_sem=rsem,
            device_id=dev, device_id_type=MESH,
        )
        copy.start()
        sent.append((src, ssem))

    def send_quiet(src, dst, ssem, rsem, dev):
        pltpu.make_async_remote_copy(
            src_ref=src, dst_ref=dst, send_sem=ssem, recv_sem=rsem,
            device_id=dev, device_id_type=MESH,
        ).start()

    own = pltpu.make_async_copy(hidden_ref, hid.at[me_s], loc.at[0])
    own.start()
    tload = pltpu.make_async_copy(teacher_hbm, tv, loc.at[1])
    tload.start()
    hload = pltpu.make_async_copy(head_hbm, head, loc.at[2])
    hload.start()

    barrier = pltpu.get_barrier_semaphore()

    def greet_dp(i, _):
        pl.semaphore_signal(
            barrier, inc=1, device_id={"dp": (me_s + i) % n_dp}, device_id_type=MESH
        )
        return 0

    def greet_v(i, _):
        pl.semaphore_signal(
            barrier, inc=1, device_id={"vocab": (me_v + i) % n_v}, device_id_type=MESH
        )
        return 0

    def shift(j):
        return j // (2 * nzh), (j // 2) % nzh, j % 2

    def moved(j, sign):
        dx, dz, dc = shift(j)
        to_x, to_z, to_c = (x + nx + sign * dx) % nx, (zh + nzh + sign * dz) % nzh, (c + dc) % 2
        to_y, to_l = (y + ny + sign * (2 * dx + dc)) % ny, (zl + dz) % 2
        return 2 * to_y + to_l, (to_x * nzh + to_z) * 2 + to_c

    def greet_source(j, _):
        pl.semaphore_signal(barrier, inc=1, device_id=moved(j, -1), device_id_type=MESH)
        return 0

    lax.fori_loop(1, n_v, greet_source, 0)
    lax.fori_loop(1, n_dp, greet_dp, 0)
    lax.fori_loop(1, n_v, greet_v, 0)
    tload.wait()

    def flip(k, _):
        tt[k] = jnp.transpose(tv[:, pl.ds(pl.multiple_of(k * 128, 128), 128)])
        return 0

    lax.fori_loop(0, n_v, flip, 0)

    final = order_ref[me_v]

    def stage_piece(k, _):
        dx = (final // (2 * nzh) + nx - k // (2 * nzh)) % nx
        dz = ((final // 2) % nzh + nzh - (k // 2) % nzh) % nzh
        dc = (final % 2 + k % 2) % 2
        picked[k] = tt[2 * (2 * ((y + 2 * dx + dc) % ny) + (zl + dz) % 2) + dz // 2]
        return 0

    lax.fori_loop(0, n_v, stage_piece, 0)
    pl.semaphore_wait(barrier, n_dp + 2 * n_v - 3)

    send(hidden_ref.at[rows(base, 32), :], reg1(me_s, base, 32), zs.at[0], zr.at[0], z_peer)

    def y_rows(g, d):
        return (base, 32) if d < half else (base + 16 * g, 16)

    for g in range(2):
        st, ct = y_rows(g, 1)
        send(hidden_ref.at[rows(st, ct), :], reg1(me_s, st, ct),
             ys.at[g, 0], yr.at[g, 0], y_nbr[g])

    def t2_step(j, _):
        k = (me_v + j) % n_v
        send_quiet(picked.at[k], qq.at[me_v], t2s.at[0], t2r.at[0], {"vocab": k})
        return 0

    lax.fori_loop(1, n_v, t2_step, 0)
    qq[me_v] = picked[me_v]

    def inverse_of(v, _):
        found = order_ref[0] * 0
        for b in range(n_v):
            found = jnp.maximum(found, jnp.where(order_ref[b] == v, b, 0))
        inv[v] = found
        return 0

    lax.fori_loop(0, n_v, inverse_of, 0)
    def t3_all():
        wait(qq.at[pl.ds(0, n_v - 1)], t2r.at[0])

        def body(j, _):
            to_s, v = moved(j, 1)
            ww[v] = qq[inv[v]]
            slot = 2 * me_s + shift(j)[1] // 2
            send_quiet(ww.at[v], tgt.at[slot], t3s.at[0], t3r.at[0], (to_s, v))
            return 0

        lax.fori_loop(1, n_v, body, 0)
        tgt[2 * me_s] = qq[inv[me_v]]

    def teacher_stats():
        def mx(i, acc):
            return jnp.maximum(acc, tt[i].astype(F32))

        top = lax.fori_loop(1, n_v, mx, tt[0].astype(F32))
        top = jnp.max(top, axis=0, keepdims=True)

        def sm(i, acc):
            return acc + jnp.exp(tt[i].astype(F32) - top)

        total = lax.fori_loop(0, n_v, sm, jnp.zeros((128, 128), F32))
        tile2[2:3, :] = top
        tile2[3:4, :] = jnp.sum(total, axis=0, keepdims=True)

    def block_y(idx):
        d = (idx + 1) // 2
        return (y + ny - d) % ny if idx % 2 == 1 else (y + d) % ny

    def block_id(g, d):
        return 2 * d - 1 if g == 0 or d == half else 2 * d

    def shard(idx, j):
        yb = block_y(idx)
        return 2 * yb + zl if j == 0 else 2 * yb + 1 - zl

    def send_x(idx, j, q):
        part = reg1(shard(idx, j), base + 16 * q, 16)
        k = 2 * idx + j
        send(part, part, xs.at[q, k], xr.at[q, k], x_nbr[q])

    def send_core(idx, kind):
        st = base if kind == 0 else obase
        part = reg1(other, st, 32) if idx == 0 else reg2(block_y(idx), st, 32)
        send(part, part, cs.at[kind, idx], cr.at[kind, idx], sib)

    def y_recv(d):
        if d == 0:
            wait(reg1(other, base, 32), zr.at[0])
            for g in range(2):
                st, ct = y_rows(g, 1)
                part = reg1(other, st, ct)
                send(part, part, ys.at[g, 1], yr.at[g, 1], y_nbr[g])
            for q in range(2):
                send_x(0, 1, q)
            send_core(0, 0)
            return
        for j in range(2):
            for g in range(2):
                idx = block_id(g, d)
                st, ct = y_rows(g, d)
                wait(reg1(shard(idx, j), st, ct), yr.at[g, 2 * (d - 1) + j])
                if d < half:
                    st, ct = y_rows(g, d + 1)
                    part = reg1(shard(idx, j), st, ct)
                    send(part, part, ys.at[g, 2 * d + j], yr.at[g, 2 * d + j], y_nbr[g])
                    for q in range(2):
                        send_x(idx, j, q)
                else:
                    send_x(idx, j, g)
        for idx in blocks_at(d):
            send_core(idx, 0)

    def blocks_at(d):
        return (0,) if d == 0 else ((2 * d - 1, 2 * d) if d < half else (2 * d - 1,))

    def x_recv(d):
        for idx in blocks_at(d):
            for j in range(2):
                for q in range(2):
                    if idx > 0 or j > 0:
                        wait(reg1(shard(idx, j), obase + 16 * q, 16), xr.at[q, 2 * idx + j])
            send_core(idx, 1)

    def compute(idx):
        yb = block_y(idx)
        for kind in range(2):
            st = base_sib if kind == 0 else obase_sib
            part = reg1(other, st, 32) if idx == 0 else reg2(yb, st, 32)
            wait(part, cr.at[kind, idx])
        block = hid[pl.ds(2 * yb, 2)].reshape(256, d_model)
        scores = lax.dot_general(
            head[...], block, (((1,), (1,)), ((), ())), preferred_element_type=F32
        )
        cols = pl.ds(pl.multiple_of(yb * 256, 256), 256)
        sc[:, cols] = scores
        top = jnp.max(scores, axis=0, keepdims=True)
        e = jnp.exp(scores - top)
        ex[:, cols] = e
        total = jnp.sum(e, axis=0, keepdims=True)
        for j in range(2):
            lanes = slice(128 * j, 128 * j + 128)
            src1[2 * yb + j, 0:1, :] = top[:, lanes]
            src1[2 * yb + j, 1:2, :] = total[:, lanes]

    own.wait()
    hload.wait()
    for stage in range(half + 3):
        if stage <= half:
            y_recv(stage)
        if stage == 0:
            teacher_stats()
        if 1 <= stage <= half + 1:
            x_recv(stage - 1)
        if stage >= 2:
            for idx in blocks_at(stage - 2):
                compute(idx)
        if stage == half - 1:
            t3_all()

    def spread_dp(src, dst, k):
        def body(i, _):
            s = (me_s + i) % n_dp
            send_quiet(src.at[s], dst.at[me_s], as_.at[k], ar_.at[k], {"dp": s})
            return 0

        lax.fori_loop(1, n_dp, body, 0)
        dst[me_s] = src[me_s]

    def share_v(tile, dst, k):
        def body(i, _):
            send_quiet(tile, dst.at[me_v], as_.at[k], ar_.at[k], {"vocab": (me_v + i) % n_v})
            return 0

        lax.fori_loop(1, n_v, body, 0)
        dst[me_v] = tile[...]

    def share_dp(tile, dst, k):
        def body(i, _):
            send_quiet(tile, dst.at[me_s], as_.at[k], ar_.at[k], {"dp": (me_s + i) % n_dp})
            return 0

        lax.fori_loop(1, n_dp, body, 0)
        dst[me_s] = tile[...]

    def merge(ref, r):
        tops = ref[:, r, :]
        sums = ref[:, r + 1, :]
        top = jnp.max(tops, axis=0, keepdims=True)
        return top, jnp.sum(sums * jnp.exp(tops - top), axis=0, keepdims=True)

    spread_dp(src1, ar1, 0)
    wait(ar1.at[pl.ds(0, n_dp - 1)], ar_.at[0])
    tile2[0:1, :], tile2[1:2, :] = merge(ar1, 0)
    share_v(tile2, ar2, 1)
    wait(ar2.at[pl.ds(0, n_v - 1)], ar_.at[1])
    tile3[0:1, :], tile3[1:2, :] = merge(ar2, 0)
    tile3[2:3, :], tile3[3:4, :] = merge(ar2, 2)
    share_dp(tile3, fin, 2)
    wait(fin.at[pl.ds(0, n_dp - 1)], ar_.at[2])

    wait(tgt.at[pl.ds(0, n_v - 1)], t3r.at[0])

    def grad_chunk(s, _):
        cols = pl.ds(pl.multiple_of(s * 128, 128), 128)
        f = fin[s]
        m_s, z_s, m_t, z_t = f[0:1], f[1:2], f[2:3], f[3:4]
        w = weight_ref[s]
        scale_s = w * jnp.exp(src1[s][0:1] - m_s) / z_s
        scale_t = w / z_t
        cross = jnp.zeros((1, 128), F32)
        for h in range(2):
            t = tgt[2 * s + h].astype(F32)
            e_t = jnp.exp(t - m_t)
            band = slice(128 * h, 128 * h + 128)
            cross = cross + jnp.sum(e_t * (t - sc[band, cols]), axis=0, keepdims=True)
            pr[band, cols] = (ex[band, cols] * scale_s - e_t * scale_t).astype(BF16)
        csrc1[s] = cross
        return 0

    lax.fori_loop(0, n_dp, grad_chunk, 0)

    n_tiles = d_model // 256

    def gemm(lo, hi):
        def body(n, _):
            cols = pl.ds(pl.multiple_of(n * 256, 256), 256)
            b = hid[:, :, cols].reshape(n_dp * 128, 256)
            grad_ref[:, cols] = jnp.dot(pr[...], b, preferred_element_type=F32).astype(BF16)
            return 0

        lax.fori_loop(lo, hi, body, 0)

    cut1, cut2 = n_tiles // 3, 2 * n_tiles // 3
    spread_dp(csrc1, car1, 3)
    gemm(0, cut1)
    wait(car1.at[pl.ds(0, n_dp - 1)], ar_.at[3])
    ctile2[...] = jnp.sum(car1[...], axis=0)
    share_v(ctile2, car2, 4)
    gemm(cut1, cut2)
    wait(car2.at[pl.ds(0, n_v - 1)], ar_.at[4])
    ctile3[...] = jnp.sum(car2[...], axis=0)
    share_dp(ctile3, cfin, 5)
    gemm(cut2, n_tiles)
    wait(cfin.at[pl.ds(0, n_dp - 1)], ar_.at[5])
    m_s, z_s, m_t, z_t = fin[:, 0, :], fin[:, 1, :], fin[:, 2, :], fin[:, 3, :]
    div_ref[...] = cfin[:, 0, :] / z_t - m_t - jnp.log(z_t) + m_s + jnp.log(z_s)

    for ref, sem in sent:
        wait(ref, sem)
    wait(picked.at[pl.ds(0, n_v - 1)], t2s.at[0])
    wait(ww.at[pl.ds(0, n_v - 1)], t3s.at[0])
    for k, ref in ((0, ar1), (1, ar2), (2, fin), (3, car1), (4, car2), (5, cfin)):
        wait(ref.at[pl.ds(0, (n_v if k % 3 == 1 else n_dp) - 1)], as_.at[k])


def on_device(nx, ny, nzh, hidden, head, teacher, shard_order, loss_weight):
    n_dp, n_v = 2 * ny, 2 * nx * nzh
    d_model = hidden.shape[1]
    tokens = n_dp * 128
    any_ = pl.BlockSpec(memory_space=pl.ANY)
    vmem = pl.BlockSpec(memory_space=pltpu.VMEM)
    smem = pl.BlockSpec(memory_space=pltpu.SMEM)
    dma = pltpu.SemaphoreType.DMA

    def stat(n, r):
        return pltpu.VMEM((n, r, 128), F32)

    tile4, tile1 = pltpu.VMEM((4, 128), F32), pltpu.VMEM((1, 128), F32)
    pieces = pltpu.VMEM((n_v, 128, 128), BF16)
    grad, div = pl.pallas_call(
        functools.partial(kernel, nx, ny, nzh),
        out_shape=(
            jax.ShapeDtypeStruct((SUB, d_model), BF16),
            jax.ShapeDtypeStruct((n_dp, 128), F32),
        ),
        in_specs=[smem, any_, any_, any_, vmem],
        out_specs=(vmem, vmem),
        scratch_shapes=[
            pltpu.SMEM((n_v,), jnp.int32),
            pltpu.VMEM((n_dp, 128, d_model), BF16),
            pltpu.VMEM((SUB, d_model), BF16),
            pltpu.VMEM((128, n_dp * SUB), BF16),
            pieces, pieces, pieces, pieces, pieces,
            pltpu.VMEM((SUB, tokens), F32),
            pltpu.VMEM((SUB, tokens), F32),
            pltpu.VMEM((SUB, tokens), BF16),
            stat(n_dp, 2), stat(n_dp, 2), tile4, stat(n_v, 4), tile4, stat(n_dp, 4),
            stat(n_dp, 1), stat(n_dp, 1), tile1, stat(n_v, 1), tile1, stat(n_dp, 1),
            dma((3,)),
            dma((1,)), dma((1,)),
            dma((2, ny)), dma((2, ny)),
            dma((2, 2 * ny)), dma((2, 2 * ny)),
            dma((2, ny)), dma((2, ny)),
            dma((1,)), dma((1,)),
            dma((1,)), dma((1,)),
            dma((6,)), dma((6,)),
        ],
        compiler_params=pltpu.CompilerParams(
            collective_id=0, has_side_effects=True, vmem_limit_bytes=56 * 1024 * 1024
        ),
        cost_estimate=pl.CostEstimate(
            flops=4 * SUB * tokens * d_model, bytes_accessed=8 * SUB * d_model, transcendentals=0
        ),
    )(shard_order, hidden, head[0], teacher, loss_weight.reshape(n_dp, 1, 128))
    return grad[None], div.reshape(tokens)


def build(mesh, nx, ny, nzh):
    in_specs = (P("dp", None), P("dp", "vocab", None), P("dp", "vocab"), P(), P())
    out_specs = (P("dp", "vocab", None), P())
    return jax.shard_map(
        functools.partial(on_device, nx, ny, nzh),
        mesh=mesh, in_specs=in_specs, out_specs=out_specs, check_vma=False,
    )


def solution(mesh):
    return build(mesh, 4, mesh.shape["dp"] // 2, mesh.shape["vocab"] // 8)
```

```python
import functools

import jax
import jax.numpy as jnp
from jax import lax
from jax.experimental import pallas as pl
from jax.experimental.pallas import tpu as pltpu
from jax.sharding import PartitionSpec as P

F32 = jnp.float32
BF16 = jnp.bfloat16
MESH = pl.DeviceIdType.MESH
SUB = 256


def rem(a, b):
    return lax.rem(a, jnp.int32(b))


def div(a, b):
    return lax.div(a, jnp.int32(b))


def kernel(
    nx, ny, nzh,
    order_ref, hidden_ref, head_hbm, teacher_hbm, weight_ref,
    grad_ref, div_ref,
    inv, hid, head, tv, tt, picked, qq, ww, tgt, sc, ex, et, pr,
    src1, ar1, tile2, ar2, tile3, fin,
    csrc1, car1, ctile2, car2, ctile3, cfin,
    loc, zs, zr, ys, yr, xs, xr, cs, cr, t2s, t2r, t3s, t3r, as_, ar_,
):
    half = ny // 2
    n_dp = 2 * ny
    n_v = 2 * nx * nzh
    d_model = hid.shape[-1]
    me_s = lax.axis_index("dp")
    me_v = lax.axis_index("vocab")
    y, zl = div(me_s, 2), rem(me_s, 2)
    x, zh, c = div(me_v, 2 * nzh), rem(div(me_v, 2), nzh), rem(me_v, 2)
    xp = rem(x, 2)
    other = 2 * y + 1 - zl
    y_nbr = [{"dp": rem(y + 1, ny) * 2 + zl}, {"dp": rem(y + ny - 1, ny) * 2 + zl}]
    x_nbr = [
        {"vocab": rem(x + 1, nx) * (2 * nzh) + rem(me_v, 2 * nzh)},
        {"vocab": rem(x + nx - 1, nx) * (2 * nzh) + rem(me_v, 2 * nzh)},
    ]
    sib = {"vocab": me_v + 1 - 2 * c}
    z_peer = {"dp": other}
    base = xp * 64 + c * 32
    obase = (1 - xp) * 64 + c * 32
    base_sib = xp * 64 + (1 - c) * 32
    obase_sib = (1 - xp) * 64 + (1 - c) * 32

    def rows(start, count):
        return pl.ds(pl.multiple_of(start, 16), count)

    def reg2(yb, start, count):
        return hid.at[pl.ds(2 * yb, 2), rows(start, count), :]

    def reg1(s, start, count):
        return hid.at[s, rows(start, count), :]

    def wait(ref, sem):
        pltpu.make_async_copy(ref, ref, sem).wait()

    sent = []

    def send(src, dst, ssem, rsem, dev):
        copy = pltpu.make_async_remote_copy(
            src_ref=src, dst_ref=dst, send_sem=ssem, recv_sem=rsem,
            device_id=dev, device_id_type=MESH,
        )
        copy.start()
        sent.append((src, ssem))

    def send_quiet(src, dst, ssem, rsem, dev):
        pltpu.make_async_remote_copy(
            src_ref=src, dst_ref=dst, send_sem=ssem, recv_sem=rsem,
            device_id=dev, device_id_type=MESH,
        ).start()

    own = pltpu.make_async_copy(hidden_ref, hid.at[me_s], loc.at[0])
    own.start()
    tload = pltpu.make_async_copy(teacher_hbm, tv, loc.at[1])
    tload.start()
    hload = pltpu.make_async_copy(head_hbm, head, loc.at[2])
    hload.start()

    barrier = pltpu.get_barrier_semaphore()

    def greet_dp(i, _):
        pl.semaphore_signal(
            barrier, inc=1, device_id={"dp": rem(me_s + i, n_dp)}, device_id_type=MESH
        )
        return 0

    def greet_v(i, _):
        pl.semaphore_signal(
            barrier, inc=1, device_id={"vocab": rem(me_v + i, n_v)}, device_id_type=MESH
        )
        return 0

    def shift(j):
        return div(j, 2 * nzh), rem(div(j, 2), nzh), rem(j, 2)

    def moved(j, sign):
        dx, dz, dc = shift(j)
        to_x, to_z, to_c = rem(x + nx + sign * dx, nx), rem(zh + nzh + sign * dz, nzh), rem(c + dc, 2)
        to_y, to_l = rem(y + ny + sign * (2 * dx + dc), ny), rem(zl + dz, 2)
        return 2 * to_y + to_l, (to_x * nzh + to_z) * 2 + to_c

    def greet_source(j, _):
        pl.semaphore_signal(barrier, inc=1, device_id=moved(j, -1), device_id_type=MESH)
        return 0

    lax.fori_loop(1, n_v, greet_source, 0)
    lax.fori_loop(1, n_dp, greet_dp, 0)
    lax.fori_loop(1, n_v, greet_v, 0)
    tload.wait()

    def flip(k, _):
        tt[k] = jnp.transpose(tv[:, pl.ds(pl.multiple_of(k * 128, 128), 128)])
        return 0

    lax.fori_loop(0, n_v, flip, 0)

    final = order_ref[me_v]

    def stage_piece(k, _):
        dx = rem(div(final, 2 * nzh) + nx - div(k, 2 * nzh), nx)
        dz = rem(rem(div(final, 2), nzh) + nzh - rem(div(k, 2), nzh), nzh)
        dc = rem(rem(final, 2) + rem(k, 2), 2)
        picked[k] = tt[2 * (2 * rem(y + 2 * dx + dc, ny) + rem(zl + dz, 2)) + div(dz, 2)]
        return 0

    lax.fori_loop(0, n_v, stage_piece, 0)
    pl.semaphore_wait(barrier, n_dp + 2 * n_v - 3)

    send(hidden_ref.at[rows(base, 32), :], reg1(me_s, base, 32), zs.at[0], zr.at[0], z_peer)

    def y_rows(g, d):
        return (base, 32) if d < half else (base + 16 * g, 16)

    for g in range(2):
        st, ct = y_rows(g, 1)
        send(hidden_ref.at[rows(st, ct), :], reg1(me_s, st, ct),
             ys.at[g, 0], yr.at[g, 0], y_nbr[g])

    def t2_step(j, _):
        k = rem(me_v + j, n_v)
        send_quiet(picked.at[k], qq.at[me_v], t2s.at[0], t2r.at[0], {"vocab": k})
        return 0

    lax.fori_loop(1, n_v, t2_step, 0)
    qq[me_v] = picked[me_v]

    def inverse_of(v, _):
        found = order_ref[0] * 0
        for b in range(n_v):
            found = jnp.maximum(found, jnp.where(order_ref[b] == v, b, 0))
        inv[v] = found
        return 0

    lax.fori_loop(0, n_v, inverse_of, 0)
    def t3_all():
        wait(qq.at[pl.ds(0, n_v - 1)], t2r.at[0])

        def body(j, _):
            to_s, v = moved(j, 1)
            ww[v] = qq[inv[v]]
            slot = 2 * me_s + div(shift(j)[1], 2)
            send_quiet(ww.at[v], tgt.at[slot], t3s.at[0], t3r.at[0], (to_s, v))
            return 0

        lax.fori_loop(1, n_v, body, 0)
        tgt[2 * me_s] = qq[inv[me_v]]

    def teacher_stats():
        def mx(i, acc):
            return jnp.maximum(acc, tt[i].astype(F32))

        top = lax.fori_loop(1, n_v, mx, tt[0].astype(F32))
        top = jnp.max(top, axis=0, keepdims=True)

        def sm(i, acc):
            return acc + jnp.exp(tt[i].astype(F32) - top)

        total = lax.fori_loop(0, n_v, sm, jnp.zeros((128, 128), F32))
        tile2[2:3, :] = top
        tile2[3:4, :] = jnp.sum(total, axis=0, keepdims=True)

    def block_y(idx):
        d = (idx + 1) // 2
        return rem(y + ny - d, ny) if idx % 2 == 1 else rem(y + d, ny)

    def block_id(g, d):
        return 2 * d - 1 if g == 0 or d == half else 2 * d

    def shard(idx, j):
        yb = block_y(idx)
        return 2 * yb + zl if j == 0 else 2 * yb + 1 - zl

    def send_x(idx, j, q):
        part = reg1(shard(idx, j), base + 16 * q, 16)
        k = 2 * idx + j
        send(part, part, xs.at[q, k], xr.at[q, k], x_nbr[q])

    def send_core(idx, kind):
        st = base if kind == 0 else obase
        part = reg1(other, st, 32) if idx == 0 else reg2(block_y(idx), st, 32)
        send(part, part, cs.at[kind, idx], cr.at[kind, idx], sib)

    def y_recv(d):
        if d == 0:
            wait(reg1(other, base, 32), zr.at[0])
            for g in range(2):
                st, ct = y_rows(g, 1)
                part = reg1(other, st, ct)
                send(part, part, ys.at[g, 1], yr.at[g, 1], y_nbr[g])
            for q in range(2):
                send_x(0, 1, q)
            send_core(0, 0)
            return
        for j in range(2):
            for g in range(2):
                idx = block_id(g, d)
                st, ct = y_rows(g, d)
                wait(reg1(shard(idx, j), st, ct), yr.at[g, 2 * (d - 1) + j])
                if d < half:
                    st, ct = y_rows(g, d + 1)
                    part = reg1(shard(idx, j), st, ct)
                    send(part, part, ys.at[g, 2 * d + j], yr.at[g, 2 * d + j], y_nbr[g])
                    for q in range(2):
                        send_x(idx, j, q)
                else:
                    send_x(idx, j, g)
        for idx in blocks_at(d):
            send_core(idx, 0)

    def blocks_at(d):
        return (0,) if d == 0 else ((2 * d - 1, 2 * d) if d < half else (2 * d - 1,))

    def x_recv(d):
        for idx in blocks_at(d):
            for j in range(2):
                for q in range(2):
                    if idx > 0 or j > 0:
                        wait(reg1(shard(idx, j), obase + 16 * q, 16), xr.at[q, 2 * idx + j])
            send_core(idx, 1)

    def compute(idx):
        yb = block_y(idx)
        for kind in range(2):
            st = base_sib if kind == 0 else obase_sib
            part = reg1(other, st, 32) if idx == 0 else reg2(yb, st, 32)
            wait(part, cr.at[kind, idx])
        block = hid[pl.ds(2 * yb, 2)].reshape(256, d_model)
        scores = lax.dot_general(
            head[...], block, (((1,), (1,)), ((), ())), preferred_element_type=F32
        )
        cols = pl.ds(pl.multiple_of(yb * 256, 256), 256)
        sc[:, cols] = scores
        top = jnp.max(scores, axis=0, keepdims=True)
        e = jnp.exp(scores - top)
        ex[:, cols] = e
        total = jnp.sum(e, axis=0, keepdims=True)
        for j in range(2):
            lanes = slice(128 * j, 128 * j + 128)
            src1[2 * yb + j, 0:1, :] = top[:, lanes]
            src1[2 * yb + j, 1:2, :] = total[:, lanes]

    own.wait()
    hload.wait()
    for stage in range(half + 3):
        if stage <= half:
            y_recv(stage)
        if stage == 0:
            teacher_stats()
        if 1 <= stage <= half + 1:
            x_recv(stage - 1)
        if stage >= 2:
            for idx in blocks_at(stage - 2):
                compute(idx)
        if stage == half - 1:
            t3_all()

    def spread_dp(src, dst, k):
        def body(i, _):
            s = rem(me_s + i, n_dp)
            send_quiet(src.at[s], dst.at[me_s], as_.at[k], ar_.at[k], {"dp": s})
            return 0

        lax.fori_loop(1, n_dp, body, 0)
        dst[me_s] = src[me_s]

    def share_v(tile, dst, k):
        def body(i, _):
            send_quiet(tile, dst.at[me_v], as_.at[k], ar_.at[k], {"vocab": rem(me_v + i, n_v)})
            return 0

        lax.fori_loop(1, n_v, body, 0)
        dst[me_v] = tile[...]

    def share_dp(tile, dst, k):
        def body(i, _):
            send_quiet(tile, dst.at[me_s], as_.at[k], ar_.at[k], {"dp": rem(me_s + i, n_dp)})
            return 0

        lax.fori_loop(1, n_dp, body, 0)
        dst[me_s] = tile[...]

    def merge(ref, r):
        tops = ref[:, r, :]
        sums = ref[:, r + 1, :]
        top = jnp.max(tops, axis=0, keepdims=True)
        return top, jnp.sum(sums * jnp.exp(tops - top), axis=0, keepdims=True)

    def target_chunk(s, _):
        cols = pl.ds(pl.multiple_of(s * 128, 128), 128)
        t = [tgt[2 * s + h].astype(F32) for h in range(2)]
        top = jnp.max(jnp.maximum(t[0], t[1]), axis=0, keepdims=True)
        cross = jnp.zeros((1, 128), F32)
        for h in range(2):
            band = slice(128 * h, 128 * h + 128)
            e_t = jnp.exp(t[h] - top)
            et[band, cols] = e_t
            cross = cross + jnp.sum(e_t * (t[h] - sc[band, cols]), axis=0, keepdims=True)
        csrc1[s, 0:1, :] = top
        csrc1[s, 1:2, :] = cross
        return 0

    def grad_chunk(s, _):
        cols = pl.ds(pl.multiple_of(s * 128, 128), 128)
        f = fin[s]
        m_s, z_s, m_t, z_t = f[0:1], f[1:2], f[2:3], f[3:4]
        w = weight_ref[s]
        scale_s = w * jnp.exp(src1[s][0:1] - m_s) / z_s
        scale_t = w * jnp.exp(csrc1[s][0:1] - m_t) / z_t
        for h in range(2):
            band = slice(128 * h, 128 * h + 128)
            pr[band, cols] = (ex[band, cols] * scale_s - et[band, cols] * scale_t).astype(BF16)
        return 0

    n_tiles = d_model // 256

    def gemm(lo, hi):
        def body(n, _):
            cols = pl.ds(pl.multiple_of(n * 256, 256), 256)
            b = hid[:, :, cols].reshape(n_dp * 128, 256)
            grad_ref[:, cols] = jnp.dot(pr[...], b, preferred_element_type=F32).astype(BF16)
            return 0

        lax.fori_loop(lo, hi, body, 0)

    spread_dp(src1, ar1, 0)
    wait(ar1.at[pl.ds(0, n_dp - 1)], ar_.at[0])
    tile2[0:1, :], tile2[1:2, :] = merge(ar1, 0)
    share_v(tile2, ar2, 1)
    wait(tgt.at[pl.ds(0, n_v - 1)], t3r.at[0])
    lax.fori_loop(0, n_dp, target_chunk, 0)
    spread_dp(csrc1, car1, 3)
    wait(ar2.at[pl.ds(0, n_v - 1)], ar_.at[1])
    tile3[0:1, :], tile3[1:2, :] = merge(ar2, 0)
    tile3[2:3, :], tile3[3:4, :] = merge(ar2, 2)
    share_dp(tile3, fin, 2)
    wait(car1.at[pl.ds(0, n_dp - 1)], ar_.at[3])
    ctile2[0:1, :], ctile2[1:2, :] = merge(car1, 0)
    share_v(ctile2, car2, 4)
    wait(fin.at[pl.ds(0, n_dp - 1)], ar_.at[2])
    lax.fori_loop(0, n_dp, grad_chunk, 0)
    cut = n_tiles // 3
    gemm(0, cut)
    wait(car2.at[pl.ds(0, n_v - 1)], ar_.at[4])
    ctile3[0:1, :], ctile3[1:2, :] = merge(car2, 0)
    share_dp(ctile3, cfin, 5)
    gemm(cut, n_tiles)
    wait(cfin.at[pl.ds(0, n_dp - 1)], ar_.at[5])
    m_s, z_s, m_t, z_t = fin[:, 0, :], fin[:, 1, :], fin[:, 2, :], fin[:, 3, :]
    div_ref[...] = cfin[:, 1, :] / z_t - m_t - jnp.log(z_t) + m_s + jnp.log(z_s)

    for ref, sem in sent:
        wait(ref, sem)
    wait(picked.at[pl.ds(0, n_v - 1)], t2s.at[0])
    wait(ww.at[pl.ds(0, n_v - 1)], t3s.at[0])
    for k, ref in ((0, ar1), (1, ar2), (2, fin), (3, car1), (4, car2), (5, cfin)):
        wait(ref.at[pl.ds(0, (n_v if k % 3 == 1 else n_dp) - 1)], as_.at[k])


def on_device(nx, ny, nzh, hidden, head, teacher, shard_order, loss_weight):
    n_dp, n_v = 2 * ny, 2 * nx * nzh
    d_model = hidden.shape[1]
    tokens = n_dp * 128
    any_ = pl.BlockSpec(memory_space=pl.ANY)
    vmem = pl.BlockSpec(memory_space=pltpu.VMEM)
    smem = pl.BlockSpec(memory_space=pltpu.SMEM)
    dma = pltpu.SemaphoreType.DMA

    def stat(n, r):
        return pltpu.VMEM((n, r, 128), F32)

    tile4, tile2 = pltpu.VMEM((4, 128), F32), pltpu.VMEM((2, 128), F32)
    pieces = pltpu.VMEM((n_v, 128, 128), BF16)
    grad, div = pl.pallas_call(
        functools.partial(kernel, nx, ny, nzh),
        out_shape=(
            jax.ShapeDtypeStruct((SUB, d_model), BF16),
            jax.ShapeDtypeStruct((n_dp, 128), F32),
        ),
        in_specs=[smem, any_, any_, any_, vmem],
        out_specs=(vmem, vmem),
        scratch_shapes=[
            pltpu.SMEM((n_v,), jnp.int32),
            pltpu.VMEM((n_dp, 128, d_model), BF16),
            pltpu.VMEM((SUB, d_model), BF16),
            pltpu.VMEM((128, n_dp * SUB), BF16),
            pieces, pieces, pieces, pieces, pieces,
            pltpu.VMEM((SUB, tokens), F32),
            pltpu.VMEM((SUB, tokens), F32),
            pltpu.VMEM((SUB, tokens), F32),
            pltpu.VMEM((SUB, tokens), BF16),
            stat(n_dp, 2), stat(n_dp, 2), tile4, stat(n_v, 4), tile4, stat(n_dp, 4),
            stat(n_dp, 2), stat(n_dp, 2), tile2, stat(n_v, 2), tile2, stat(n_dp, 2),
            dma((3,)),
            dma((1,)), dma((1,)),
            dma((2, ny)), dma((2, ny)),
            dma((2, 2 * ny)), dma((2, 2 * ny)),
            dma((2, ny)), dma((2, ny)),
            dma((1,)), dma((1,)),
            dma((1,)), dma((1,)),
            dma((6,)), dma((6,)),
        ],
        compiler_params=pltpu.CompilerParams(
            collective_id=0, has_side_effects=True, vmem_limit_bytes=56 * 1024 * 1024
        ),
        cost_estimate=pl.CostEstimate(
            flops=4 * SUB * tokens * d_model, bytes_accessed=8 * SUB * d_model, transcendentals=0
        ),
    )(shard_order, hidden, head[0], teacher, loss_weight.reshape(n_dp, 1, 128))
    return grad[None], div.reshape(tokens)


def build(mesh, nx, ny, nzh):
    in_specs = (P("dp", None), P("dp", "vocab", None), P("dp", "vocab"), P(), P())
    out_specs = (P("dp", "vocab", None), P())
    return jax.shard_map(
        functools.partial(on_device, nx, ny, nzh),
        mesh=mesh, in_specs=in_specs, out_specs=out_specs, check_vma=False,
    )


def solution(mesh):
    return build(mesh, 4, mesh.shape["dp"] // 2, mesh.shape["vocab"] // 8)
```

```python
import functools

import jax
import jax.numpy as jnp
from jax import lax
from jax.experimental import pallas as pl
from jax.experimental.pallas import tpu as pltpu
from jax.sharding import PartitionSpec as P

F32 = jnp.float32
BF16 = jnp.bfloat16
MESH = pl.DeviceIdType.MESH
SUB = 256
HANDOVERS = 2


def rem(a, b):
    return lax.rem(a, jnp.int32(b))


def div(a, b):
    return lax.div(a, jnp.int32(b))


def kernel(
    nx, ny, nzh,
    order_ref, hidden_ref, head_hbm, teacher_hbm, weight_ref,
    grad_ref, div_ref,
    inv, hid, head, tv, tt, picked, qq, ww, tgt, sc, ex, et, pr,
    src1, ar1, tile2, ar2, tile3, fin,
    csrc1, car1, ctile2, car2, ctile3, cfin,
    loc, zs, zr, ys, yr, xs, xr, cs, cr, t2s, t2r, t3s, t3r, as_, ar_,
):
    half = ny // 2
    n_dp = 2 * ny
    n_v = 2 * nx * nzh
    d_model = hid.shape[-1]
    me_s = lax.axis_index("dp")
    me_v = lax.axis_index("vocab")
    y, zl = div(me_s, 2), rem(me_s, 2)
    x, zh, c = div(me_v, 2 * nzh), rem(div(me_v, 2), nzh), rem(me_v, 2)
    xp = rem(x, 2)
    other = 2 * y + 1 - zl
    y_nbr = [{"dp": rem(y + 1, ny) * 2 + zl}, {"dp": rem(y + ny - 1, ny) * 2 + zl}]
    x_nbr = [
        {"vocab": rem(x + 1, nx) * (2 * nzh) + rem(me_v, 2 * nzh)},
        {"vocab": rem(x + nx - 1, nx) * (2 * nzh) + rem(me_v, 2 * nzh)},
    ]
    sib = {"vocab": me_v + 1 - 2 * c}
    z_peer = {"dp": other}
    base = xp * 64 + c * 32
    obase = (1 - xp) * 64 + c * 32
    base_sib = xp * 64 + (1 - c) * 32
    obase_sib = (1 - xp) * 64 + (1 - c) * 32

    def rows(start, count):
        return pl.ds(pl.multiple_of(start, 16), count)

    def reg2(yb, start, count):
        return hid.at[pl.ds(2 * yb, 2), rows(start, count), :]

    def reg1(s, start, count):
        return hid.at[s, rows(start, count), :]

    def wait(ref, sem):
        pltpu.make_async_copy(ref, ref, sem).wait()

    sent = []

    def send(src, dst, ssem, rsem, dev):
        copy = pltpu.make_async_remote_copy(
            src_ref=src, dst_ref=dst, send_sem=ssem, recv_sem=rsem,
            device_id=dev, device_id_type=MESH,
        )
        copy.start()
        sent.append((src, ssem))

    def send_quiet(src, dst, ssem, rsem, dev):
        pltpu.make_async_remote_copy(
            src_ref=src, dst_ref=dst, send_sem=ssem, recv_sem=rsem,
            device_id=dev, device_id_type=MESH,
        ).start()

    own = pltpu.make_async_copy(hidden_ref, hid.at[me_s], loc.at[0])
    own.start()
    tload = pltpu.make_async_copy(teacher_hbm, tv, loc.at[1])
    tload.start()
    hload = pltpu.make_async_copy(head_hbm, head, loc.at[2])
    hload.start()

    barrier = pltpu.get_barrier_semaphore()

    def greet_dp(i, _):
        pl.semaphore_signal(
            barrier, inc=1, device_id={"dp": rem(me_s + i, n_dp)}, device_id_type=MESH
        )
        return 0

    def greet_v(i, _):
        pl.semaphore_signal(
            barrier, inc=1, device_id={"vocab": rem(me_v + i, n_v)}, device_id_type=MESH
        )
        return 0

    def shift(j):
        return div(j, 2 * nzh), rem(div(j, 2), nzh), rem(j, 2)

    def moved(j, sign):
        dx, dz, dc = shift(j)
        to_x, to_z, to_c = rem(x + nx + sign * dx, nx), rem(zh + nzh + sign * dz, nzh), rem(c + dc, 2)
        to_y, to_l = rem(y + ny + sign * (2 * dx + dc), ny), rem(zl + dz, 2)
        return 2 * to_y + to_l, (to_x * nzh + to_z) * 2 + to_c

    def greet_source(j, _):
        pl.semaphore_signal(barrier, inc=1, device_id=moved(j, -1), device_id_type=MESH)
        return 0

    lax.fori_loop(1, n_v, greet_source, 0)
    lax.fori_loop(1, n_dp, greet_dp, 0)
    lax.fori_loop(1, n_v, greet_v, 0)
    tload.wait()

    def flip(k, _):
        tt[k] = jnp.transpose(tv[:, pl.ds(pl.multiple_of(k * 128, 128), 128)])
        return 0

    lax.fori_loop(0, n_v, flip, 0)

    final = order_ref[me_v]

    def stage_piece(k, _):
        dx = rem(div(final, 2 * nzh) + nx - div(k, 2 * nzh), nx)
        dz = rem(rem(div(final, 2), nzh) + nzh - rem(div(k, 2), nzh), nzh)
        dc = rem(rem(final, 2) + rem(k, 2), 2)
        picked[k] = tt[2 * (2 * rem(y + 2 * dx + dc, ny) + rem(zl + dz, 2)) + div(dz, 2)]
        return 0

    lax.fori_loop(0, n_v, stage_piece, 0)
    pl.semaphore_wait(barrier, n_dp + 2 * n_v - 3)

    send(hidden_ref.at[rows(base, 32), :], reg1(me_s, base, 32), zs.at[0], zr.at[0], z_peer)

    def y_rows(g, d):
        return (base, 32) if d < half else (base + 16 * g, 16)

    for g in range(2):
        st, ct = y_rows(g, 1)
        send(hidden_ref.at[rows(st, ct), :], reg1(me_s, st, ct),
             ys.at[g, 0], yr.at[g, 0], y_nbr[g])

    def t2_step(j, _):
        k = rem(me_v + j, n_v)
        send_quiet(picked.at[k], qq.at[me_v], t2s.at[0], t2r.at[0], {"vocab": k})
        return 0


    def inverse_of(v, _):
        found = order_ref[0] * 0
        for b in range(n_v):
            found = jnp.maximum(found, jnp.where(order_ref[b] == v, b, 0))
        inv[v] = found
        return 0

    lax.fori_loop(0, n_v, inverse_of, 0)
    def t3_all():
        wait(qq.at[pl.ds(0, n_v - 1)], t2r.at[0])

        def body(j, _):
            to_s, v = moved(j, 1)
            ww[v] = qq[inv[v]]
            slot = 2 * me_s + div(shift(j)[1], 2)
            send_quiet(ww.at[v], tgt.at[slot], t3s.at[0], t3r.at[0], (to_s, v))
            return 0

        lax.fori_loop(1, n_v, body, 0)
        tgt[2 * me_s] = qq[inv[me_v]]

    def teacher_stats():
        def mx(i, acc):
            return jnp.maximum(acc, tt[i].astype(F32))

        top = lax.fori_loop(1, n_v, mx, tt[0].astype(F32))
        top = jnp.max(top, axis=0, keepdims=True)

        def sm(i, acc):
            return acc + jnp.exp(tt[i].astype(F32) - top)

        total = lax.fori_loop(0, n_v, sm, jnp.zeros((128, 128), F32))
        tile2[2:3, :] = top
        tile2[3:4, :] = jnp.sum(total, axis=0, keepdims=True)

    def block_y(idx):
        d = (idx + 1) // 2
        return rem(y + ny - d, ny) if idx % 2 == 1 else rem(y + d, ny)

    def block_id(g, d):
        return 2 * d - 1 if g == 0 or d == half else 2 * d

    def shard(idx, j):
        yb = block_y(idx)
        return 2 * yb + zl if j == 0 else 2 * yb + 1 - zl

    def send_x(idx, j, q):
        part = reg1(shard(idx, j), base + 16 * q, 16)
        k = 2 * idx + j
        send(part, part, xs.at[q, k], xr.at[q, k], x_nbr[q])

    def send_core(idx, kind):
        st = base if kind == 0 else obase
        part = reg1(other, st, 32) if idx == 0 else reg2(block_y(idx), st, 32)
        send(part, part, cs.at[kind, idx], cr.at[kind, idx], sib)

    def y_recv(d):
        if d == 0:
            wait(reg1(other, base, 32), zr.at[0])
            for g in range(2):
                st, ct = y_rows(g, 1)
                part = reg1(other, st, ct)
                send(part, part, ys.at[g, 1], yr.at[g, 1], y_nbr[g])
            for q in range(2):
                send_x(0, 1, q)
            send_core(0, 0)
            return
        for j in range(2):
            for g in range(2):
                idx = block_id(g, d)
                st, ct = y_rows(g, d)
                wait(reg1(shard(idx, j), st, ct), yr.at[g, 2 * (d - 1) + j])
                if d < half:
                    st, ct = y_rows(g, d + 1)
                    part = reg1(shard(idx, j), st, ct)
                    send(part, part, ys.at[g, 2 * d + j], yr.at[g, 2 * d + j], y_nbr[g])
                    for q in range(2):
                        send_x(idx, j, q)
                else:
                    send_x(idx, j, g)
        for idx in blocks_at(d):
            send_core(idx, 0)

    def blocks_at(d):
        return (0,) if d == 0 else ((2 * d - 1, 2 * d) if d < half else (2 * d - 1,))

    def x_recv(d):
        for idx in blocks_at(d):
            for j in range(2):
                for q in range(2):
                    if idx > 0 or j > 0:
                        wait(reg1(shard(idx, j), obase + 16 * q, 16), xr.at[q, 2 * idx + j])
            send_core(idx, 1)

    def compute(idx):
        yb = block_y(idx)
        for kind in range(2):
            st = base_sib if kind == 0 else obase_sib
            part = reg1(other, st, 32) if idx == 0 else reg2(yb, st, 32)
            wait(part, cr.at[kind, idx])
        block = hid[pl.ds(2 * yb, 2)].reshape(256, d_model)
        scores = lax.dot_general(
            head[...], block, (((1,), (1,)), ((), ())), preferred_element_type=F32
        )
        cols = pl.ds(pl.multiple_of(yb * 256, 256), 256)
        sc[:, cols] = scores
        top = jnp.max(scores, axis=0, keepdims=True)
        e = jnp.exp(scores - top)
        ex[:, cols] = e
        total = jnp.sum(e, axis=0, keepdims=True)
        for j in range(2):
            lanes = slice(128 * j, 128 * j + 128)
            src1[2 * yb + j, 0:1, :] = top[:, lanes]
            src1[2 * yb + j, 1:2, :] = total[:, lanes]

    own.wait()
    hload.wait()
    for stage in range(half + 3):
        if stage <= half:
            y_recv(stage)
        if stage == 0:
            lax.fori_loop(1, n_v, t2_step, 0)
            qq[me_v] = picked[me_v]
        if 1 <= stage <= half + 1:
            x_recv(stage - 1)
        if stage >= 2:
            for idx in blocks_at(stage - 2):
                compute(idx)
        if stage == half - 1:
            t3_all()
            teacher_stats()

    def spread_dp(src, dst, k):
        def body(i, _):
            s = rem(me_s + i, n_dp)
            send_quiet(src.at[s], dst.at[me_s], as_.at[k], ar_.at[k], {"dp": s})
            return 0

        lax.fori_loop(1, n_dp, body, 0)
        dst[me_s] = src[me_s]

    def share_v(tile, dst, k):
        def body(i, _):
            send_quiet(tile, dst.at[me_v], as_.at[k], ar_.at[k], {"vocab": rem(me_v + i, n_v)})
            return 0

        lax.fori_loop(1, n_v, body, 0)
        dst[me_v] = tile[...]

    def share_dp(tile, dst, k):
        def body(i, _):
            send_quiet(tile, dst.at[me_s], as_.at[k], ar_.at[k], {"dp": rem(me_s + i, n_dp)})
            return 0

        lax.fori_loop(1, n_dp, body, 0)
        dst[me_s] = tile[...]

    def merge(ref, r):
        tops = ref[:, r, :]
        sums = ref[:, r + 1, :]
        top = jnp.max(tops, axis=0, keepdims=True)
        return top, jnp.sum(sums * jnp.exp(tops - top), axis=0, keepdims=True)

    def target_chunk(s, _):
        cols = pl.ds(pl.multiple_of(s * 128, 128), 128)
        t = [tgt[2 * s + h].astype(F32) for h in range(2)]
        top = jnp.max(jnp.maximum(t[0], t[1]), axis=0, keepdims=True)
        cross = jnp.zeros((1, 128), F32)
        for h in range(2):
            band = slice(128 * h, 128 * h + 128)
            e_t = jnp.exp(t[h] - top)
            et[band, cols] = e_t
            cross = cross + jnp.sum(e_t * (t[h] - sc[band, cols]), axis=0, keepdims=True)
        csrc1[s, 0:1, :] = top
        csrc1[s, 1:2, :] = cross
        return 0

    def grad_chunk(s, _):
        cols = pl.ds(pl.multiple_of(s * 128, 128), 128)
        f = fin[s]
        m_s, z_s, m_t, z_t = f[0:1], f[1:2], f[2:3], f[3:4]
        w = weight_ref[s]
        scale_s = w * jnp.exp(src1[s][0:1] - m_s) / z_s
        scale_t = w * jnp.exp(csrc1[s][0:1] - m_t) / z_t
        for h in range(2):
            band = slice(128 * h, 128 * h + 128)
            pr[band, cols] = (ex[band, cols] * scale_s - et[band, cols] * scale_t).astype(BF16)
        return 0

    n_tiles = d_model // 256

    def gemm(lo, hi):
        def body(n, _):
            cols = pl.ds(pl.multiple_of(n * 256, 256), 256)
            b = hid[:, :, cols].reshape(n_dp * 128, 256)
            grad_ref[:, cols] = jnp.dot(pr[...], b, preferred_element_type=F32).astype(BF16)
            return 0

        lax.fori_loop(lo, hi, body, 0)

    spread_dp(src1, ar1, 0)
    wait(ar1.at[pl.ds(0, n_dp - 1)], ar_.at[0])
    tile2[0:1, :], tile2[1:2, :] = merge(ar1, 0)
    share_v(tile2, ar2, 1)
    wait(tgt.at[pl.ds(0, n_v - 1)], t3r.at[0])
    lax.fori_loop(0, n_dp, target_chunk, 0)
    spread_dp(csrc1, car1, 3)
    wait(ar2.at[pl.ds(0, n_v - 1)], ar_.at[1])
    tile3[0:1, :], tile3[1:2, :] = merge(ar2, 0)
    tile3[2:3, :], tile3[3:4, :] = merge(ar2, 2)
    share_dp(tile3, fin, 2)
    wait(car1.at[pl.ds(0, n_dp - 1)], ar_.at[3])
    ctile2[0:1, :], ctile2[1:2, :] = merge(car1, 0)
    share_v(ctile2, car2, 4)
    wait(fin.at[pl.ds(0, n_dp - 1)], ar_.at[2])
    lax.fori_loop(0, n_dp, grad_chunk, 0)
    cut = n_tiles // 3
    gemm(0, cut)
    wait(car2.at[pl.ds(0, n_v - 1)], ar_.at[4])
    ctile3[0:1, :], ctile3[1:2, :] = merge(car2, 0)
    share_dp(ctile3, cfin, 5)
    gemm(cut, n_tiles)
    wait(cfin.at[pl.ds(0, n_dp - 1)], ar_.at[5])
    m_s, z_s, m_t, z_t = fin[:, 0, :], fin[:, 1, :], fin[:, 2, :], fin[:, 3, :]
    div_ref[...] = cfin[:, 1, :] / z_t - m_t - jnp.log(z_t) + m_s + jnp.log(z_s)

    for ref, sem in sent:
        wait(ref, sem)
    wait(picked.at[pl.ds(0, n_v - 1)], t2s.at[0])
    wait(ww.at[pl.ds(0, n_v - 1)], t3s.at[0])
    for k, ref in ((0, ar1), (1, ar2), (2, fin), (3, car1), (4, car2), (5, cfin)):
        wait(ref.at[pl.ds(0, (n_v if k % 3 == 1 else n_dp) - 1)], as_.at[k])


def hand_over(grad_ref, div_ref, grad_out, div_out):
    grad_out[...] = grad_ref[...]
    div_out[...] = div_ref[...]


def on_device(nx, ny, nzh, hidden, head, teacher, shard_order, loss_weight):
    n_dp, n_v = 2 * ny, 2 * nx * nzh
    d_model = hidden.shape[1]
    tokens = n_dp * 128
    any_ = pl.BlockSpec(memory_space=pl.ANY)
    vmem = pl.BlockSpec(memory_space=pltpu.VMEM)
    smem = pl.BlockSpec(memory_space=pltpu.SMEM)
    dma = pltpu.SemaphoreType.DMA

    def stat(n, r):
        return pltpu.VMEM((n, r, 128), F32)

    tile4, tile2 = pltpu.VMEM((4, 128), F32), pltpu.VMEM((2, 128), F32)
    pieces = pltpu.VMEM((n_v, 128, 128), BF16)
    grad, div = pl.pallas_call(
        functools.partial(kernel, nx, ny, nzh),
        out_shape=(
            jax.ShapeDtypeStruct((SUB, d_model), BF16),
            jax.ShapeDtypeStruct((n_dp, 128), F32),
        ),
        in_specs=[smem, any_, any_, any_, vmem],
        out_specs=(vmem, vmem),
        scratch_shapes=[
            pltpu.SMEM((n_v,), jnp.int32),
            pltpu.VMEM((n_dp, 128, d_model), BF16),
            pltpu.VMEM((SUB, d_model), BF16),
            pltpu.VMEM((128, n_dp * SUB), BF16),
            pieces, pieces, pieces, pieces, pieces,
            pltpu.VMEM((SUB, tokens), F32),
            pltpu.VMEM((SUB, tokens), F32),
            pltpu.VMEM((SUB, tokens), F32),
            pltpu.VMEM((SUB, tokens), BF16),
            stat(n_dp, 2), stat(n_dp, 2), tile4, stat(n_v, 4), tile4, stat(n_dp, 4),
            stat(n_dp, 2), stat(n_dp, 2), tile2, stat(n_v, 2), tile2, stat(n_dp, 2),
            dma((3,)),
            dma((1,)), dma((1,)),
            dma((2, ny)), dma((2, ny)),
            dma((2, 2 * ny)), dma((2, 2 * ny)),
            dma((2, ny)), dma((2, ny)),
            dma((1,)), dma((1,)),
            dma((1,)), dma((1,)),
            dma((6,)), dma((6,)),
        ],
        compiler_params=pltpu.CompilerParams(
            collective_id=0, has_side_effects=True, vmem_limit_bytes=56 * 1024 * 1024
        ),
        cost_estimate=pl.CostEstimate(
            flops=4 * SUB * tokens * d_model, bytes_accessed=8 * SUB * d_model, transcendentals=0
        ),
    )(shard_order, hidden, head[0], teacher, loss_weight.reshape(n_dp, 1, 128))
    band = pl.BlockSpec((SUB // HANDOVERS, d_model), lambda i: (i, 0))
    whole = pl.BlockSpec((n_dp, 128), lambda i: (0, 0))
    grad, div = pl.pallas_call(
        hand_over,
        grid=(HANDOVERS,),
        out_shape=(
            jax.ShapeDtypeStruct((SUB, d_model), BF16),
            jax.ShapeDtypeStruct((n_dp, 128), F32),
        ),
        in_specs=[band, whole],
        out_specs=(band, whole),
    )(grad, div)
    return grad[None], div.reshape(tokens)


def build(mesh, nx, ny, nzh):
    in_specs = (P("dp", None), P("dp", "vocab", None), P("dp", "vocab"), P(), P())
    out_specs = (P("dp", "vocab", None), P())
    return jax.shard_map(
        functools.partial(on_device, nx, ny, nzh),
        mesh=mesh, in_specs=in_specs, out_specs=out_specs, check_vma=False,
    )


def solution(mesh):
    return build(mesh, 4, mesh.shape["dp"] // 2, mesh.shape["vocab"] // 8)
```

```python
import functools

import jax
import jax.numpy as jnp
from jax import lax
from jax.experimental import pallas as pl
from jax.experimental.pallas import tpu as pltpu
from jax.sharding import PartitionSpec as P

F32 = jnp.float32
BF16 = jnp.bfloat16
MESH = pl.DeviceIdType.MESH
SUB = 256
HANDOVERS = 2


def rem(a, b):
    return lax.rem(a, jnp.int32(b))


def div(a, b):
    return lax.div(a, jnp.int32(b))


def kernel(
    nx, ny, nzh,
    order_ref, hidden_ref, head_hbm, teacher_hbm, weight_ref,
    grad_ref, div_ref,
    inv, hid, head, tv, tt, picked, qq, ww, tgt, sc, ex, et, pr,
    src1, ar1, tile2, ar2, tile3, fin,
    csrc1, car1, ctile2, car2, ctile3, cfin,
    loc, zs, zr, ys, yr, xs, xr, cs, cr, t2s, t2r, t3s, t3r, as_, ar_,
):
    half = ny // 2
    n_dp = 2 * ny
    n_v = 2 * nx * nzh
    d_model = hid.shape[-1]
    me_s = lax.axis_index("dp")
    me_v = lax.axis_index("vocab")
    y, zl = div(me_s, 2), rem(me_s, 2)
    x, zh, c = div(me_v, 2 * nzh), rem(div(me_v, 2), nzh), rem(me_v, 2)
    xp = rem(x, 2)
    other = 2 * y + 1 - zl
    y_nbr = [{"dp": rem(y + 1, ny) * 2 + zl}, {"dp": rem(y + ny - 1, ny) * 2 + zl}]
    x_nbr = [
        {"vocab": rem(x + 1, nx) * (2 * nzh) + rem(me_v, 2 * nzh)},
        {"vocab": rem(x + nx - 1, nx) * (2 * nzh) + rem(me_v, 2 * nzh)},
    ]
    sib = {"vocab": me_v + 1 - 2 * c}
    z_peer = {"dp": other}
    base = xp * 64 + c * 32
    obase = (1 - xp) * 64 + c * 32
    base_sib = xp * 64 + (1 - c) * 32
    obase_sib = (1 - xp) * 64 + (1 - c) * 32

    def rows(start, count):
        return pl.ds(pl.multiple_of(start, 16), count)

    def reg2(yb, start, count):
        return hid.at[pl.ds(2 * yb, 2), rows(start, count), :]

    def reg1(s, start, count):
        return hid.at[s, rows(start, count), :]

    def wait(ref, sem):
        pltpu.make_async_copy(ref, ref, sem).wait()

    sent = []

    def send(src, dst, ssem, rsem, dev):
        copy = pltpu.make_async_remote_copy(
            src_ref=src, dst_ref=dst, send_sem=ssem, recv_sem=rsem,
            device_id=dev, device_id_type=MESH,
        )
        copy.start()
        sent.append((src, ssem))

    def send_quiet(src, dst, ssem, rsem, dev):
        pltpu.make_async_remote_copy(
            src_ref=src, dst_ref=dst, send_sem=ssem, recv_sem=rsem,
            device_id=dev, device_id_type=MESH,
        ).start()

    own = pltpu.make_async_copy(hidden_ref, hid.at[me_s], loc.at[0])
    own.start()
    tload = pltpu.make_async_copy(teacher_hbm, tv, loc.at[1])
    tload.start()
    hload = pltpu.make_async_copy(head_hbm, head, loc.at[2])
    hload.start()

    barrier = pltpu.get_barrier_semaphore()

    def greet_dp(i, _):
        pl.semaphore_signal(
            barrier, inc=1, device_id={"dp": rem(me_s + i, n_dp)}, device_id_type=MESH
        )
        return 0

    def greet_v(i, _):
        pl.semaphore_signal(
            barrier, inc=1, device_id={"vocab": rem(me_v + i, n_v)}, device_id_type=MESH
        )
        return 0

    def shift(j):
        return div(j, 2 * nzh), rem(div(j, 2), nzh), rem(j, 2)

    def moved(j, sign):
        dx, dz, dc = shift(j)
        to_x, to_z, to_c = rem(x + nx + sign * dx, nx), rem(zh + nzh + sign * dz, nzh), rem(c + dc, 2)
        to_y, to_l = rem(y + ny + sign * (2 * dx + dc), ny), rem(zl + dz, 2)
        return 2 * to_y + to_l, (to_x * nzh + to_z) * 2 + to_c

    def greet_source(j, _):
        pl.semaphore_signal(barrier, inc=1, device_id=moved(j, -1), device_id_type=MESH)
        return 0

    lax.fori_loop(1, n_v, greet_source, 0)
    lax.fori_loop(1, n_dp, greet_dp, 0)
    lax.fori_loop(1, n_v, greet_v, 0)
    tload.wait()

    def flip(k, _):
        tt[k] = jnp.transpose(tv[:, pl.ds(pl.multiple_of(k * 128, 128), 128)])
        return 0

    lax.fori_loop(0, n_v, flip, 0)

    final = order_ref[me_v]

    def stage_piece(k, _):
        dx = rem(div(final, 2 * nzh) + nx - div(k, 2 * nzh), nx)
        dz = rem(rem(div(final, 2), nzh) + nzh - rem(div(k, 2), nzh), nzh)
        dc = rem(rem(final, 2) + rem(k, 2), 2)
        picked[k] = tt[2 * (2 * rem(y + 2 * dx + dc, ny) + rem(zl + dz, 2)) + div(dz, 2)]
        return 0

    lax.fori_loop(0, n_v, stage_piece, 0)
    pl.semaphore_wait(barrier, n_dp + 2 * n_v - 3)

    send(hidden_ref.at[rows(base, 32), :], reg1(me_s, base, 32), zs.at[0], zr.at[0], z_peer)

    def y_rows(g, d):
        return (base, 32) if d < half else (base + 16 * g, 16)

    for g in range(2):
        st, ct = y_rows(g, 1)
        send(hidden_ref.at[rows(st, ct), :], reg1(me_s, st, ct),
             ys.at[g, 0], yr.at[g, 0], y_nbr[g])

    def t2_send(m, dz):
        to_x, to_z, to_c = rem(x + div(m, 2), nx), rem(zh + dz, nzh), rem(c + rem(m, 2), 2)
        k = (to_x * nzh + to_z) * 2 + to_c
        send_quiet(picked.at[k], qq.at[me_v], t2s.at[0], t2r.at[0], {"vocab": k})

    def t2_near(m, _):
        t2_send(m, 0)
        return 0

    def t2_far(i, _):
        t2_send(rem(i, 2 * nx), 1 + div(i, 2 * nx))
        return 0

    lax.fori_loop(1, 2 * nx, t2_near, 0)

    def inverse_of(v, _):
        found = order_ref[0] * 0
        for b in range(n_v):
            found = jnp.maximum(found, jnp.where(order_ref[b] == v, b, 0))
        inv[v] = found
        return 0

    lax.fori_loop(0, n_v, inverse_of, 0)
    def t3_all():
        wait(qq.at[pl.ds(0, n_v - 1)], t2r.at[0])

        def body(j, _):
            to_s, v = moved(j, 1)
            ww[v] = qq[inv[v]]
            slot = 2 * me_s + div(shift(j)[1], 2)
            send_quiet(ww.at[v], tgt.at[slot], t3s.at[0], t3r.at[0], (to_s, v))
            return 0

        lax.fori_loop(1, n_v, body, 0)
        tgt[2 * me_s] = qq[inv[me_v]]

    def teacher_stats():
        def mx(i, acc):
            return jnp.maximum(acc, tt[i].astype(F32))

        top = lax.fori_loop(1, n_v, mx, tt[0].astype(F32))
        top = jnp.max(top, axis=0, keepdims=True)

        def sm(i, acc):
            return acc + jnp.exp(tt[i].astype(F32) - top)

        total = lax.fori_loop(0, n_v, sm, jnp.zeros((128, 128), F32))
        tile2[2:3, :] = top
        tile2[3:4, :] = jnp.sum(total, axis=0, keepdims=True)

    def block_y(idx):
        d = (idx + 1) // 2
        return rem(y + ny - d, ny) if idx % 2 == 1 else rem(y + d, ny)

    def block_id(g, d):
        return 2 * d - 1 if g == 0 or d == half else 2 * d

    def shard(idx, j):
        yb = block_y(idx)
        return 2 * yb + zl if j == 0 else 2 * yb + 1 - zl

    def send_x(idx, j, q):
        part = reg1(shard(idx, j), base + 16 * q, 16)
        k = 2 * idx + j
        send(part, part, xs.at[q, k], xr.at[q, k], x_nbr[q])

    def send_core(idx, kind):
        st = base if kind == 0 else obase
        part = reg1(other, st, 32) if idx == 0 else reg2(block_y(idx), st, 32)
        send(part, part, cs.at[kind, idx], cr.at[kind, idx], sib)

    def y_recv(d):
        if d == 0:
            wait(reg1(other, base, 32), zr.at[0])
            for g in range(2):
                st, ct = y_rows(g, 1)
                part = reg1(other, st, ct)
                send(part, part, ys.at[g, 1], yr.at[g, 1], y_nbr[g])
            for q in range(2):
                send_x(0, 1, q)
            send_core(0, 0)
            return
        for j in range(2):
            for g in range(2):
                idx = block_id(g, d)
                st, ct = y_rows(g, d)
                wait(reg1(shard(idx, j), st, ct), yr.at[g, 2 * (d - 1) + j])
                if d < half:
                    st, ct = y_rows(g, d + 1)
                    part = reg1(shard(idx, j), st, ct)
                    send(part, part, ys.at[g, 2 * d + j], yr.at[g, 2 * d + j], y_nbr[g])
                    for q in range(2):
                        send_x(idx, j, q)
                else:
                    send_x(idx, j, g)
        for idx in blocks_at(d):
            send_core(idx, 0)

    def blocks_at(d):
        return (0,) if d == 0 else ((2 * d - 1, 2 * d) if d < half else (2 * d - 1,))

    def x_recv(d):
        for idx in blocks_at(d):
            for j in range(2):
                for q in range(2):
                    if idx > 0 or j > 0:
                        wait(reg1(shard(idx, j), obase + 16 * q, 16), xr.at[q, 2 * idx + j])
            send_core(idx, 1)

    def compute(idx):
        yb = block_y(idx)
        for kind in range(2):
            st = base_sib if kind == 0 else obase_sib
            part = reg1(other, st, 32) if idx == 0 else reg2(yb, st, 32)
            wait(part, cr.at[kind, idx])
        block = hid[pl.ds(2 * yb, 2)].reshape(256, d_model)
        scores = lax.dot_general(
            head[...], block, (((1,), (1,)), ((), ())), preferred_element_type=F32
        )
        cols = pl.ds(pl.multiple_of(yb * 256, 256), 256)
        sc[:, cols] = scores
        top = jnp.max(scores, axis=0, keepdims=True)
        e = jnp.exp(scores - top)
        ex[:, cols] = e
        total = jnp.sum(e, axis=0, keepdims=True)
        for j in range(2):
            lanes = slice(128 * j, 128 * j + 128)
            src1[2 * yb + j, 0:1, :] = top[:, lanes]
            src1[2 * yb + j, 1:2, :] = total[:, lanes]

    own.wait()
    hload.wait()
    for stage in range(half + 3):
        if stage <= half:
            y_recv(stage)
        if stage == 0:
            lax.fori_loop(0, 2 * nx * (nzh - 1), t2_far, 0)
            qq[me_v] = picked[me_v]
        if 1 <= stage <= half + 1:
            x_recv(stage - 1)
        if stage >= 2:
            for idx in blocks_at(stage - 2):
                compute(idx)
        if stage == half - 1:
            t3_all()
            teacher_stats()

    def spread_dp(src, dst, k):
        def body(i, _):
            s = rem(me_s + i, n_dp)
            send_quiet(src.at[s], dst.at[me_s], as_.at[k], ar_.at[k], {"dp": s})
            return 0

        lax.fori_loop(1, n_dp, body, 0)
        dst[me_s] = src[me_s]

    def share_v(tile, dst, k):
        def body(i, _):
            send_quiet(tile, dst.at[me_v], as_.at[k], ar_.at[k], {"vocab": rem(me_v + i, n_v)})
            return 0

        lax.fori_loop(1, n_v, body, 0)
        dst[me_v] = tile[...]

    def share_dp(tile, dst, k):
        def body(i, _):
            send_quiet(tile, dst.at[me_s], as_.at[k], ar_.at[k], {"dp": rem(me_s + i, n_dp)})
            return 0

        lax.fori_loop(1, n_dp, body, 0)
        dst[me_s] = tile[...]

    def merge(ref, r):
        tops = ref[:, r, :]
        sums = ref[:, r + 1, :]
        top = jnp.max(tops, axis=0, keepdims=True)
        return top, jnp.sum(sums * jnp.exp(tops - top), axis=0, keepdims=True)

    def target_chunk(s, _):
        cols = pl.ds(pl.multiple_of(s * 128, 128), 128)
        t = [tgt[2 * s + h].astype(F32) for h in range(2)]
        top = jnp.max(jnp.maximum(t[0], t[1]), axis=0, keepdims=True)
        cross = jnp.zeros((1, 128), F32)
        for h in range(2):
            band = slice(128 * h, 128 * h + 128)
            e_t = jnp.exp(t[h] - top)
            et[band, cols] = e_t
            cross = cross + jnp.sum(e_t * (t[h] - sc[band, cols]), axis=0, keepdims=True)
        csrc1[s, 0:1, :] = top
        csrc1[s, 1:2, :] = cross
        return 0

    def grad_chunk(s, _):
        cols = pl.ds(pl.multiple_of(s * 128, 128), 128)
        f = fin[s]
        m_s, z_s, m_t, z_t = f[0:1], f[1:2], f[2:3], f[3:4]
        w = weight_ref[s]
        scale_s = w * jnp.exp(src1[s][0:1] - m_s) / z_s
        scale_t = w * jnp.exp(csrc1[s][0:1] - m_t) / z_t
        for h in range(2):
            band = slice(128 * h, 128 * h + 128)
            pr[band, cols] = (ex[band, cols] * scale_s - et[band, cols] * scale_t).astype(BF16)
        return 0

    n_tiles = d_model // 256

    def gemm(lo, hi):
        def body(n, _):
            cols = pl.ds(pl.multiple_of(n * 256, 256), 256)
            b = hid[:, :, cols].reshape(n_dp * 128, 256)
            grad_ref[:, cols] = jnp.dot(pr[...], b, preferred_element_type=F32).astype(BF16)
            return 0

        lax.fori_loop(lo, hi, body, 0)

    spread_dp(src1, ar1, 0)
    wait(ar1.at[pl.ds(0, n_dp - 1)], ar_.at[0])
    tile2[0:1, :], tile2[1:2, :] = merge(ar1, 0)
    share_v(tile2, ar2, 1)
    wait(tgt.at[pl.ds(0, n_v - 1)], t3r.at[0])
    lax.fori_loop(0, n_dp, target_chunk, 0)
    spread_dp(csrc1, car1, 3)
    wait(ar2.at[pl.ds(0, n_v - 1)], ar_.at[1])
    tile3[0:1, :], tile3[1:2, :] = merge(ar2, 0)
    tile3[2:3, :], tile3[3:4, :] = merge(ar2, 2)
    share_dp(tile3, fin, 2)
    wait(car1.at[pl.ds(0, n_dp - 1)], ar_.at[3])
    ctile2[0:1, :], ctile2[1:2, :] = merge(car1, 0)
    share_v(ctile2, car2, 4)
    wait(fin.at[pl.ds(0, n_dp - 1)], ar_.at[2])
    lax.fori_loop(0, n_dp, grad_chunk, 0)
    cut = n_tiles // 3
    gemm(0, cut)
    wait(car2.at[pl.ds(0, n_v - 1)], ar_.at[4])
    ctile3[0:1, :], ctile3[1:2, :] = merge(car2, 0)
    share_dp(ctile3, cfin, 5)
    gemm(cut, n_tiles)
    wait(cfin.at[pl.ds(0, n_dp - 1)], ar_.at[5])
    m_s, z_s, m_t, z_t = fin[:, 0, :], fin[:, 1, :], fin[:, 2, :], fin[:, 3, :]
    div_ref[...] = cfin[:, 1, :] / z_t - m_t - jnp.log(z_t) + m_s + jnp.log(z_s)

    for ref, sem in sent:
        wait(ref, sem)
    wait(picked.at[pl.ds(0, n_v - 1)], t2s.at[0])
    wait(ww.at[pl.ds(0, n_v - 1)], t3s.at[0])
    for k, ref in ((0, ar1), (1, ar2), (2, fin), (3, car1), (4, car2), (5, cfin)):
        wait(ref.at[pl.ds(0, (n_v if k % 3 == 1 else n_dp) - 1)], as_.at[k])


def hand_over(grad_ref, div_ref, grad_out, div_out):
    grad_out[...] = grad_ref[...]
    div_out[...] = div_ref[...]


def on_device(nx, ny, nzh, hidden, head, teacher, shard_order, loss_weight):
    n_dp, n_v = 2 * ny, 2 * nx * nzh
    d_model = hidden.shape[1]
    tokens = n_dp * 128
    any_ = pl.BlockSpec(memory_space=pl.ANY)
    vmem = pl.BlockSpec(memory_space=pltpu.VMEM)
    smem = pl.BlockSpec(memory_space=pltpu.SMEM)
    dma = pltpu.SemaphoreType.DMA

    def stat(n, r):
        return pltpu.VMEM((n, r, 128), F32)

    tile4, tile2 = pltpu.VMEM((4, 128), F32), pltpu.VMEM((2, 128), F32)
    pieces = pltpu.VMEM((n_v, 128, 128), BF16)
    grad, div = pl.pallas_call(
        functools.partial(kernel, nx, ny, nzh),
        out_shape=(
            jax.ShapeDtypeStruct((SUB, d_model), BF16),
            jax.ShapeDtypeStruct((n_dp, 128), F32),
        ),
        in_specs=[smem, any_, any_, any_, vmem],
        out_specs=(vmem, vmem),
        scratch_shapes=[
            pltpu.SMEM((n_v,), jnp.int32),
            pltpu.VMEM((n_dp, 128, d_model), BF16),
            pltpu.VMEM((SUB, d_model), BF16),
            pltpu.VMEM((128, n_dp * SUB), BF16),
            pieces, pieces, pieces, pieces, pieces,
            pltpu.VMEM((SUB, tokens), F32),
            pltpu.VMEM((SUB, tokens), F32),
            pltpu.VMEM((SUB, tokens), F32),
            pltpu.VMEM((SUB, tokens), BF16),
            stat(n_dp, 2), stat(n_dp, 2), tile4, stat(n_v, 4), tile4, stat(n_dp, 4),
            stat(n_dp, 2), stat(n_dp, 2), tile2, stat(n_v, 2), tile2, stat(n_dp, 2),
            dma((3,)),
            dma((1,)), dma((1,)),
            dma((2, ny)), dma((2, ny)),
            dma((2, 2 * ny)), dma((2, 2 * ny)),
            dma((2, ny)), dma((2, ny)),
            dma((1,)), dma((1,)),
            dma((1,)), dma((1,)),
            dma((6,)), dma((6,)),
        ],
        compiler_params=pltpu.CompilerParams(
            collective_id=0, has_side_effects=True, vmem_limit_bytes=56 * 1024 * 1024
        ),
        cost_estimate=pl.CostEstimate(
            flops=4 * SUB * tokens * d_model, bytes_accessed=8 * SUB * d_model, transcendentals=0
        ),
    )(shard_order, hidden, head[0], teacher, loss_weight.reshape(n_dp, 1, 128))
    band = pl.BlockSpec((SUB // HANDOVERS, d_model), lambda i: (i, 0))
    whole = pl.BlockSpec((n_dp, 128), lambda i: (0, 0))
    grad, div = pl.pallas_call(
        hand_over,
        grid=(HANDOVERS,),
        out_shape=(
            jax.ShapeDtypeStruct((SUB, d_model), BF16),
            jax.ShapeDtypeStruct((n_dp, 128), F32),
        ),
        in_specs=[band, whole],
        out_specs=(band, whole),
    )(grad, div)
    return grad[None], div.reshape(tokens)


def build(mesh, nx, ny, nzh):
    in_specs = (P("dp", None), P("dp", "vocab", None), P("dp", "vocab"), P(), P())
    out_specs = (P("dp", "vocab", None), P())
    return jax.shard_map(
        functools.partial(on_device, nx, ny, nzh),
        mesh=mesh, in_specs=in_specs, out_specs=out_specs, check_vma=False,
    )


def solution(mesh):
    return build(mesh, 4, mesh.shape["dp"] // 2, mesh.shape["vocab"] // 8)
```
